256 devices in a mesh: pool: 64 (over z, x, core), head: 4 (over y).
Axes of the slice: x: 4, y: 4, z: 8, core: 2. Of those that a mesh axis runs over, the one named last changes fastest.
Arguments:
- hidden_rows: bfloat16 [256, 8192], P(None, 'pool'), may hold values from -48 to 48
- cache_kv: bfloat16 [64, 512, 2, 1024], P(None, 'pool', None, 'head'), may hold values from -16 to 16
- sel_index: int32 [192], replicated, may hold values from 0 to 32767, as said below
- doc_order: int32 [64], replicated, may hold values from 0 to 63, each once
- attn_gain: bfloat16 [8192], P('pool'), may hold values from 0.099609375 to 1.8984375
- w_query: bfloat16 [8192, 8192], P('pool', 'head'), may hold values from -1 to 1
- w_keyval: bfloat16 [8192, 2, 1024], P('pool', None, 'head'), may hold values from -0.1875 to 0.1875
- w_output: bfloat16 [8192, 8192], P('head', 'pool'), may hold values from -0.0625 to 0.0625
- ffn_gain: bfloat16 [8192], P('pool'), may hold values from 0.099609375 to 1.8984375
- w_in: bfloat16 [8192, 2, 28672], P(None, None, ('pool', 'head')), may hold values from -0.0625 to 0.0625
- w_out: bfloat16 [28672, 8192], P(('pool', 'head')), may hold values from -0.15625 to 0.15625
Outputs:
- layer_out: bfloat16 [256, 8192], P('head', 'pool')
- joined_cache: bfloat16 [32768, 2, 1024], P('pool', None, 'head')
The draws below stay inside these ranges and needn't reach their ends.
Inputs may be any that keep to these rules, and one draw needn't show every extreme that they name: `sel_index`: distinct values; 0 and 32767 are always present; the count per document varies.
All inputs are finite; a program needn't handle non-finite values.
Results may differ from the reference program's by a relative error of at most 0.017.
Values may be sent and summed in bfloat16 or wider, within the bound.
No kernel may reach another device: no remote copies, remote signals or barrier semaphores. Data moves between devices by JAX's collectives and lax.ppermute only.
A program may use at most 64 MiB of HBM per device.

```python
import math
import jax
import jax.numpy as jnp
from jax import lax

D = 8192
HEADS = 64
KV_HEADS = 8
HEAD_DIM = 128
FF = 28672
DOC_LEN = 512
SEL_DEV = 3
QRY_DEV = 1
DOCS = 64
SEQ = 32768
SEL = 192
QUERY = 64
ROWS = 256
N_POOL = 64


def draw_hidden_rows(key, part):
    key = jax.random.fold_in(key, 11)
    first, second, third = jax.random.split(key, 3)
    row_scale = jnp.exp(jax.random.uniform(second, (ROWS, 1), jnp.float32, math.log(0.3), math.log(3.0)))
    place = jnp.arange(D, dtype=jnp.float32) / D
    col_scale = jnp.exp(jax.random.uniform(third, (1, D), jnp.float32, math.log(0.5), math.log(2.0))) * jnp.power(3.0, place - 0.5)[None, :]
    base = jnp.clip(jax.random.normal(first, (ROWS, D), jnp.float32), -4.0, 4.0)
    return (base * row_scale * col_scale).astype(jnp.bfloat16)


def draw_w_query(key, part):
    key = jax.random.fold_in(key, 12)
    base = jnp.clip(jax.random.normal(key, (D, HEADS * HEAD_DIM), jnp.float32), -6.0, 6.0) / math.sqrt(D)
    return base.astype(jnp.bfloat16)


def draw_cache_kv(key, part):
    key = jax.random.fold_in(key, 13)
    first = jax.random.fold_in(key, 0)
    shape = (DOCS, DOC_LEN, 2, KV_HEADS * HEAD_DIM)
    base = 3.0 * jnp.clip(jax.random.normal(first, shape, jnp.float32), -5.0, 5.0)
    return base.astype(jnp.bfloat16)


def draw_sel_index(key, part):
    key = jax.random.fold_in(key, 14)
    total = DOCS * DOC_LEN
    inner = jax.random.permutation(key, total - 2)[:SEL - 2].astype(jnp.int32) + 1
    ends = jnp.array([0, total - 1], dtype=jnp.int32)
    return jnp.concatenate([ends, inner])


def strengthened(drawn, stream_key, source, target, parts, factor):
    def block_of(position):
        return (jnp.arange(drawn.shape[position]) // (drawn.shape[position] // parts)).reshape((-1,) + (1,) * (drawn.ndim - 1 - position))

    one_side = jax.random.permutation(stream_key, parts)[block_of(target)]
    far = (block_of(target) + parts // 2) % parts
    return jnp.where((block_of(source) == one_side) | (block_of(source) == far), factor * drawn, drawn)


def shard_levels(own_key, extent, pieces, least, top_value):
    def one(dim, parts):
        draws = jax.random.uniform(jax.random.fold_in(jax.random.fold_in(own_key, 6), dim), (parts,), jnp.float32, least / len(pieces), top_value / len(pieces))
        return jnp.repeat(jnp.exp(draws), extent[dim] // parts).reshape((-1,) + (1,) * (len(extent) - dim - 1))

    factor_of = one(*pieces[0])
    for cut in pieces[1:]:
        factor_of = factor_of * one(*cut)
    return factor_of


def centred(stream_key, shape, width, most, shards=(), kind=jnp.bfloat16):
    entries = width * jax.random.normal(stream_key, shape, jnp.float32)
    if shards:
        entries = entries * shard_levels(stream_key, shape, shards, -0.22, 0.18)
    return jnp.clip(entries, -most, most).astype(kind)


def heavy_noise(rng, extent, width, limit, cuts, heavy, kind=jnp.bfloat16):
    values = width * jax.random.normal(rng, extent, jnp.float32)
    if cuts:
        values = values * shard_levels(rng, extent, cuts, -0.22, 0.18)
    return jnp.clip(strengthened(values, jax.random.fold_in(rng, 3), *heavy), -limit, limit).astype(kind)


def setup_inputs(seed: int = 0) -> dict:
    key_of = jax.random.split(jax.random.key(seed), 12)
    return {
        "hidden_rows": draw_hidden_rows(jax.random.fold_in(key_of[11], 71), 0),
        "cache_kv": draw_cache_kv(jax.random.fold_in(key_of[11], 71), 0),
        "sel_index": draw_sel_index(jax.random.fold_in(key_of[11], 71), 0),
        "doc_order": jax.random.permutation(key_of[3], DOCS).astype(jnp.int32),
        "attn_gain": jnp.clip(1.0 + 0.18 * jax.random.normal(key_of[4], (D,), jnp.float32), 0.099609375, 1.8984375).astype(jnp.bfloat16),
        "w_query": draw_w_query(jax.random.fold_in(key_of[11], 71), 0),
        "w_keyval": centred(key_of[6], (D, 2, KV_HEADS * HEAD_DIM), (D // 9) ** -0.5, 0.1875, ((0, 64), (2, 4))),
        "w_output": centred(key_of[7], (HEADS * HEAD_DIM, D), (HEADS * HEAD_DIM) ** -0.5, 0.0625, ((0, 4), (1, 64))),
        "ffn_gain": jnp.clip(1.0 + 0.18 * jax.random.normal(key_of[8], (D,), jnp.float32), 0.099609375, 1.8984375).astype(jnp.bfloat16),
        "w_in": centred(key_of[9], (D, 2, FF), D ** -0.5, 0.0625, ((2, 256),)),
        "w_out": heavy_noise(key_of[10], (FF, D), FF ** -0.5, 0.15625, ((0, 256),), (0, 1, 256, 6.0)),
    }


EPS = 1e-05
NEG = -1e+30

def row_positions(sel_index, doc_order, pool):
    docs = jnp.arange(pool, dtype=jnp.int32)
    slot_of_doc = lax.optimization_barrier(jnp.sum(jnp.where(doc_order[:, None] == docs[None, :], docs[:, None], 0), axis=0)).astype(jnp.int32)
    sel_doc = (sel_index // DOC_LEN).astype(jnp.int32)
    sel_tok = (sel_index % DOC_LEN).astype(jnp.int32)
    sel_slot = lax.optimization_barrier(jnp.sum(jnp.where(sel_doc[:, None] == docs[None, :], slot_of_doc[None, :], 0), axis=1)).astype(jnp.int32)
    sel_pos = sel_slot * DOC_LEN + sel_tok
    query_pos = DOC_LEN * pool + jnp.arange(pool * QRY_DEV, dtype=jnp.int32)
    row_pos = jnp.concatenate([sel_pos.reshape(pool, SEL_DEV), query_pos.reshape(pool, QRY_DEV)], axis=1).reshape(-1)
    return (sel_slot, sel_tok, sel_pos, row_pos)

def normalize(values, gain):
    squares = lax.optimization_barrier(jnp.sum(values * values, axis=1, keepdims=True))
    return (values * lax.rsqrt(squares / D + EPS) * gain.astype(jnp.float32)[None, :]).astype(jnp.bfloat16)

def reference(hidden_rows, cache_kv, sel_index, doc_order, attn_gain, w_query, w_keyval, w_output, ffn_gain, w_in, w_out):
    kv_width = KV_HEADS * HEAD_DIM
    group = HEADS // KV_HEADS
    inputs = hidden_rows.astype(jnp.float32)
    normed = normalize(inputs, attn_gain)
    queries = jnp.dot(normed, w_query, preferred_element_type=jnp.float32).astype(jnp.bfloat16)
    new_kv = jnp.dot(normed, w_keyval.reshape(D, 2 * kv_width), preferred_element_type=jnp.float32).astype(jnp.bfloat16)
    new_kv = new_kv.reshape(N_POOL, SEL_DEV + QRY_DEV, 2, kv_width)
    sel_kv = new_kv[:, :SEL_DEV].reshape(SEL, 2, kv_width)
    query_kv = new_kv[:, SEL_DEV:].reshape(QUERY, 2, kv_width)
    sel_slot, sel_tok, sel_pos, row_pos = row_positions(sel_index, doc_order, N_POOL)
    joined = jnp.take(cache_kv, doc_order, axis=0).reshape(SEQ, 2, kv_width)
    joined = joined.at[sel_pos].set(sel_kv)
    keys_all = jnp.concatenate([joined, query_kv], axis=0)
    total_keys = SEQ + QUERY
    key_pos = jnp.arange(total_keys, dtype=jnp.int32)
    heads_kv = keys_all.reshape(total_keys, 2, KV_HEADS, HEAD_DIM).transpose(2, 1, 0, 3)
    query_heads = queries.reshape(ROWS, KV_HEADS, group, HEAD_DIM).transpose(1, 0, 2, 3)
    blocks = SEL_DEV + QRY_DEV
    scale = 1.0 / HEAD_DIM ** 0.5

    def one_head(packed):
        head_q, head_kv = packed
        keys = head_kv[0]
        values = head_kv[1]
        block_q = head_q.reshape(blocks, N_POOL * group, HEAD_DIM)
        block_pos = jnp.repeat(row_pos, group).reshape(blocks, N_POOL * group)

        def one_block(item):
            q_rows, q_pos = item
            scores = jnp.dot(q_rows, keys.T, preferred_element_type=jnp.float32) * scale
            kept = key_pos[None, :] <= q_pos[:, None]
            scores = jnp.where(kept, scores, NEG)
            top = lax.optimization_barrier(jnp.max(scores, axis=1, keepdims=True))
            probs = jnp.where(kept, jnp.exp(scores - top), 0.0)
            total = lax.optimization_barrier(jnp.sum(probs, axis=1, keepdims=True))
            weights = probs.astype(jnp.bfloat16)
            summed = jnp.dot(weights, values, preferred_element_type=jnp.float32)
            return (summed / total).astype(jnp.bfloat16)
        result = lax.map(one_block, (block_q, block_pos))
        return result.reshape(ROWS, group, HEAD_DIM)
    attended = lax.map(one_head, (query_heads, heads_kv))
    attended = attended.transpose(1, 0, 2, 3).reshape(ROWS, HEADS * HEAD_DIM)
    mid = inputs + jnp.dot(attended, w_output, preferred_element_type=jnp.float32)
    ffn_in = normalize(mid, ffn_gain)
    both = jnp.dot(ffn_in, w_in.reshape(D, 2 * FF), preferred_element_type=jnp.float32)
    act = (jax.nn.silu(both[:, :FF]) * both[:, FF:]).astype(jnp.bfloat16)
    layer_out = (mid + jnp.dot(act, w_out, preferred_element_type=jnp.float32)).astype(jnp.bfloat16)
    return (layer_out, joined)
```

```python
import functools

import jax
import jax.numpy as jnp
from jax import lax
from jax.experimental import pallas as pl
from jax.experimental.pallas import tpu as pltpu
from jax.sharding import Mesh
from jax.sharding import PartitionSpec as P

D = 8192
HEAD_DIM = 128
DOC_LEN = 512
SEL_DEV = 3
EPS = 1e-05
NEG = -1e30
FLOOR = -1e29
NZ, NX, NC, NY = 8, 4, 2, 4
POOL = NZ * NX * NC
ROWS = 256
EXT = 528

BF = jnp.bfloat16
F32 = jnp.float32


def exchange_cores(value):
    return lax.ppermute(value, "c", [(0, 1), (1, 0)])


def shift_y(value, step):
    return lax.ppermute(value, "y", [(i, (i + step) % NY) for i in range(NY)])


def permute_xy(value, target):
    pairs = []
    for x in range(NX):
        for y in range(NY):
            to_x, to_y = target(x, y)
            pairs.append((x * NY + y, (to_x % NX) * NY + to_y % NY))
    return lax.ppermute(value, ("x", "y"), pairs)


def swap_zx(value):
    return lax.all_to_all(value, ("z", "x"), 0, 0, tiled=True)


def parts_of(value):
    high = lax.reduce_precision(value, 8, 7)
    rest = value - high
    middle = lax.reduce_precision(rest, 8, 7)
    low = rest - middle
    return [high.astype(BF), middle.astype(BF), low.astype(BF)]


def positions(sel_index, doc_order, mine):
    docs = jnp.arange(POOL, dtype=jnp.int32)
    slot_of_doc = jnp.sum(jnp.where(doc_order[:, None] == docs[None, :], docs[:, None], 0), axis=0)
    sel_doc = sel_index // DOC_LEN
    sel_tok = sel_index % DOC_LEN
    sel_slot = jnp.sum(
        jnp.where(sel_doc[:, None] == docs[None, :], slot_of_doc[None, :], 0), axis=1
    )
    sel_pos = sel_slot * DOC_LEN + sel_tok
    query_pos = DOC_LEN * POOL + docs
    row_pos = jnp.concatenate([sel_pos.reshape(POOL, SEL_DEV), query_pos[:, None]], axis=1)
    sel_key = jnp.where(sel_slot == mine, sel_tok, -1)
    query_key = jnp.where(docs == mine, DOC_LEN, -1)
    row_key = jnp.concatenate([sel_key.reshape(POOL, SEL_DEV), query_key[:, None]], axis=1)
    both = jnp.stack([row_pos.reshape(ROWS), row_key.reshape(ROWS)])
    return jnp.concatenate([both, jnp.zeros((6, ROWS), jnp.int32)], axis=0)


def attend_kernel(
    place_ref, info_ref, own_ref, other_ref, cache_ref, joined_ref, acc_ref, sent_ref, stat_ref
):
    core = place_ref[0]
    mine = place_ref[1]
    row_pos = info_ref[0:1, :]
    row_key = info_ref[1:2, :]
    token = lax.broadcasted_iota(jnp.int32, (EXT, ROWS), 0)
    hit = token == row_key
    hits = jnp.where(hit, 1.0, 0.0)
    covered = jnp.max(hits, axis=1, keepdims=True) > 0.0
    hits = hits.astype(BF)
    key_pos = jnp.where(
        token < DOC_LEN,
        mine * DOC_LEN + token,
        jnp.where(token == DOC_LEN, DOC_LEN * POOL + mine, DOC_LEN * POOL * 2),
    )
    kept = key_pos <= row_pos
    nt = (((1,), (1,)), ((), ()))
    tn = (((0,), (0,)), ((), ()))
    for rel in range(2):
        new_ref = own_ref if rel == 0 else other_ref
        group = core if rel == 0 else 1 - core
        sides = []
        for side in range(2):
            new = new_ref[1024 + side * 128 : 1152 + side * 128, :]
            placed = lax.dot_general(hits, new, nt, preferred_element_type=F32).astype(BF)
            at = pl.ds(pl.multiple_of(side * 256 + group * 128, 128), 128)
            old = cache_ref[:, at]
            joined = jnp.where(covered[:DOC_LEN], placed[:DOC_LEN], old)
            joined_ref[:, at] = joined
            sides.append(jnp.concatenate([joined, placed[DOC_LEN:]], axis=0))
        keys, values = sides
        for head in range(8):
            query = new_ref[head * 128 : head * 128 + 128, :]
            scores = jnp.dot(keys, query, preferred_element_type=F32) * (HEAD_DIM**-0.5)
            scores = jnp.where(kept, scores, NEG)
            top = jnp.maximum(jnp.max(scores, axis=0, keepdims=True), FLOOR)
            probs = jnp.exp(scores - top)
            total = jnp.sum(probs, axis=0, keepdims=True)
            acc = lax.dot_general(values, probs.astype(BF), tn, preferred_element_type=F32)
            if rel == 0:
                acc_ref[head * 128 : head * 128 + 128, :] = acc
            else:
                sent_ref[head * 128 : head * 128 + 128, :] = acc.astype(BF)
            stat_ref[rel, 0, head : head + 1, :] = top
            stat_ref[rel, 1, head : head + 1, :] = total


def attend(place, info, own, other, cache):
    vmem = pl.BlockSpec(memory_space=pltpu.VMEM)
    return pl.pallas_call(
        attend_kernel,
        out_shape=(
            jax.ShapeDtypeStruct((DOC_LEN, 512), BF),
            jax.ShapeDtypeStruct((1024, ROWS), F32),
            jax.ShapeDtypeStruct((1024, ROWS), BF),
            jax.ShapeDtypeStruct((2, 2, 8, ROWS), F32),
        ),
        in_specs=[pl.BlockSpec(memory_space=pltpu.SMEM), vmem, vmem, vmem, vmem],
        out_specs=(vmem, vmem, vmem, vmem),
        compiler_params=pltpu.CompilerParams(vmem_limit_bytes=40 * 1024 * 1024),
        cost_estimate=pl.CostEstimate(
            flops=2 * 16 * 2 * EXT * 128 * 256, bytes_accessed=6_000_000, transcendentals=0
        ),
        name="attend",
    )(place, info, own, other, cache)


def shards(
    hidden_rows,
    cache_kv,
    sel_index,
    doc_order,
    attn_gain,
    w_query,
    w_keyval,
    w_output,
    ffn_gain,
    w_in,
    w_out,
):
    z, x, c, y = (lax.axis_index(name) for name in ("z", "x", "c", "y"))
    mine = (z * NX + x) * NC + c
    other = 1 - c

    def half(group):
        return jnp.concatenate(
            [
                lax.dynamic_slice_in_dim(w_query, group * 1024, 1024, 1),
                lax.dynamic_slice_in_dim(w_keyval[:, 0], group * 128, 128, 1),
                lax.dynamic_slice_in_dim(w_keyval[:, 1], group * 128, 128, 1),
            ],
            axis=1,
        )

    message = jnp.concatenate(
        [hidden_rows, jnp.broadcast_to(attn_gain[None, :], (16, 128))], axis=0
    )
    theirs = exchange_cores(message)
    weight_theirs = exchange_cores(half(other))
    weight = jnp.concatenate([half(c), weight_theirs], axis=0)
    inputs = jnp.concatenate([hidden_rows, theirs[:ROWS]], axis=1).astype(F32)
    gain = jnp.concatenate([attn_gain, theirs[ROWS]], axis=0).astype(F32)
    squares = jnp.sum(inputs * inputs, axis=1)
    scaled = (inputs * gain[None, :]).astype(BF)
    partial = lax.dot_general(
        weight, scaled, (((0,), (1,)), ((), ())), preferred_element_type=F32
    )
    square_parts = jnp.stack(parts_of(squares) + [jnp.zeros((ROWS,), BF)] * 5)
    payload = jnp.concatenate(
        [
            partial.astype(BF).reshape(32, 40, ROWS),
            jnp.broadcast_to(square_parts[None], (32, 8, ROWS)),
        ],
        axis=1,
    )
    arrived = swap_zx(payload).astype(F32)
    total = jnp.sum(arrived, axis=0)
    square_sum = total[40] + (total[41] + total[42])
    factor = lax.rsqrt(square_sum / D + EPS)
    piece = (total[:40] * factor[None, :]).astype(BF)
    own = swap_zx(jnp.broadcast_to(piece[None], (32, 40, ROWS))).reshape(1280, ROWS)
    others = exchange_cores(own)

    reordered = cache_kv.reshape(POOL, 8, 512).at[doc_order].get(mode="promise_in_bounds")
    slot_cache = lax.all_to_all(
        reordered, ("z", "x", "c"), split_axis=0, concat_axis=0, tiled=True
    ).reshape(DOC_LEN, 512)

    info = positions(sel_index, doc_order, mine)
    place = jnp.stack([c, mine]).astype(jnp.int32)
    joined, acc_own, acc_sent, stats = attend(place, info, own, others, slot_cache)

    acc_theirs = exchange_cores(acc_sent)
    stat_theirs = exchange_cores(stats[1])
    top = jnp.maximum(stats[0, 0], stat_theirs[0])
    mine_by = jnp.exp(stats[0, 0] - top)
    theirs_by = jnp.exp(stat_theirs[0] - top)
    totals = stats[0, 1] * mine_by + stat_theirs[1] * theirs_by
    merged = (
        acc_own.reshape(8, 128, ROWS) * mine_by[:, None, :]
        + acc_theirs.reshape(8, 128, ROWS).astype(F32) * theirs_by[:, None, :]
    ).astype(BF)
    stat_rows = jnp.stack(parts_of(top) + parts_of(totals) + [jnp.zeros((8, ROWS), BF)] * 2, axis=1)
    payload = jnp.concatenate(
        [
            merged.reshape(32, 32, ROWS),
            jnp.broadcast_to(stat_rows[:, None], (8, 4, 8, ROWS)).reshape(32, 8, ROWS),
        ],
        axis=1,
    )
    arrived = swap_zx(payload).astype(F32)
    tops = arrived[:, 32] + (arrived[:, 33] + arrived[:, 34])
    sums = arrived[:, 35] + (arrived[:, 36] + arrived[:, 37])
    by = jnp.exp(tops - jnp.max(tops, axis=0, keepdims=True))
    norm = jnp.sum(sums * by, axis=0)
    summed = jnp.sum(arrived[:, :32] * by[:, None, :], axis=0)
    piece = (summed / norm[None, :]).astype(BF)
    attended = swap_zx(jnp.broadcast_to(piece[None], (32, 32, ROWS))).reshape(1024, ROWS)
    attended_theirs = exchange_cores(attended)

    tn = (((0,), (0,)), ((), ()))
    out_own = lax.dynamic_slice_in_dim(w_output, c * 1024, 1024, 0)
    out_theirs = lax.dynamic_slice_in_dim(w_output, other * 1024, 1024, 0)
    projected = lax.dot_general(attended, out_own, tn, preferred_element_type=F32)
    projected = projected + lax.dot_general(
        attended_theirs, out_theirs, tn, preferred_element_type=F32
    )
    chunks = projected.astype(BF).reshape(4, 64, 128)
    early = jnp.concatenate(
        [
            lax.dynamic_slice_in_dim(hidden_rows, y * 64, 64, 0),
            jnp.broadcast_to(ffn_gain[None, :], (16, 128)),
        ],
        axis=0,
    )
    early = permute_xy(early, lambda a, b: (b, a))
    mid = early[:64].astype(F32)
    for step in range(4):
        sent = lax.dynamic_index_in_dim(chunks, (y + step) % NY, 0, keepdims=False)
        mid = mid + permute_xy(sent, lambda a, b: (b + step, a)).astype(F32)
    feature = (mid * early[64].astype(F32)[None, :]).astype(BF)
    square_parts = jnp.stack(parts_of(jnp.sum(mid * mid, axis=1)) + [jnp.zeros((64,), BF)] * 5)
    payload = jnp.concatenate([feature, jnp.pad(square_parts, ((0, 0), (0, 64)))], axis=0)
    arrived = swap_zx(jnp.broadcast_to(payload[None], (32, 72, 128)))
    arrived_theirs = exchange_cores(arrived)

    flat_in = jnp.transpose(w_in, (1, 2, 0)).reshape(224, D)

    def columns(array, step):
        start = ((y + step) % NY) * 256
        return jnp.concatenate(
            [
                lax.dynamic_slice_in_dim(array, k * 1024 + start + core * 128, 128, 1)
                for core in (c, other)
                for k in range(NZ)
            ],
            axis=1,
        )

    ins = [columns(flat_in, 0)]
    outs = [columns(w_out, 0)]
    for step in range(1, 4):
        ins.append(shift_y(columns(flat_in, step), step))
    for step in range(1, 4):
        outs.append(shift_y(columns(w_out, step), step))

    def features_of(block):
        return jnp.transpose(block[:, :64].reshape(NZ, ROWS, 128), (1, 0, 2)).reshape(ROWS, 1024)

    def squares_of(block):
        parts = jnp.sum(block[:, 64:67, :64].astype(F32), axis=1)
        return jnp.sum(parts.reshape(NZ, ROWS), axis=0)

    nt = (((1,), (1,)), ((), ()))
    feature_own = features_of(arrived)
    feature_theirs = features_of(arrived_theirs)
    square_sum = squares_of(arrived) + squares_of(arrived_theirs)
    square_rows = jnp.stack(parts_of(square_sum) + [jnp.zeros((ROWS,), BF)] * 5)
    hidden = []
    for step in range(4):
        term = lax.dot_general(
            ins[step][:, :1024], feature_own, nt, preferred_element_type=F32
        ) + lax.dot_general(
            ins[step][:, 1024:], feature_theirs, nt, preferred_element_type=F32
        )
        hidden.append(term)
    both = hidden[0]
    for step in range(1, 4):
        sent = jnp.concatenate([hidden[step].astype(BF), square_rows], axis=0)
        got = shift_y(sent, -step).astype(F32)
        both = both + got[:224]
        square_sum = square_sum + (got[224] + (got[225] + got[226]))
    both = both * lax.rsqrt(square_sum / D + EPS)[None, :]
    act = (jax.nn.silu(both[:112]) * both[112:]).astype(BF)
    acts = [act] + [shift_y(act, step) for step in range(1, 4)]
    act_all = jnp.concatenate(acts, axis=0)
    out_all = jnp.concatenate(outs, axis=0)
    term_theirs = lax.dot_general(act_all, out_all[:, 1024:], tn, preferred_element_type=F32)
    got = exchange_cores(term_theirs.astype(BF))
    term = lax.dot_general(act_all, out_all[:, :1024], tn, preferred_element_type=F32)
    term = (term + got.astype(F32)).astype(BF)
    payload = jnp.transpose(term.reshape(ROWS, NZ, 128), (1, 0, 2)).reshape(32, 64, 128)
    down = jnp.sum(swap_zx(payload).astype(F32), axis=0)
    result = permute_xy((mid + down).astype(BF), lambda a, b: (b, a))
    return (result, joined.reshape(DOC_LEN, 2, 256))


def solution(mesh):
    split = Mesh(mesh.devices.reshape(NZ, NX, NC, NY), ("z", "x", "c", "y"))
    pool = ("z", "x", "c")
    return jax.shard_map(
        shards,
        mesh=split,
        in_specs=(
            P(None, pool),
            P(None, pool, None, "y"),
            P(),
            P(),
            P(pool),
            P(pool, "y"),
            P(pool, None, "y"),
            P("y", pool),
            P(pool),
            P(None, None, ("z", "x", "c", "y")),
            P(("z", "x", "c", "y"), None),
        ),
        out_specs=(P("y", pool), P(pool, None, "y")),
        check_vma=False,
    )
```

```python
import functools

import jax
import jax.numpy as jnp
from jax import lax
from jax.experimental import pallas as pl
from jax.experimental.pallas import tpu as pltpu
from jax.sharding import Mesh
from jax.sharding import PartitionSpec as P

D = 8192
HEAD_DIM = 128
DOC_LEN = 512
SEL_DEV = 3
EPS = 1e-05
NEG = -1e30
FLOOR = -1e29
NZ, NX, NC, NY = 8, 4, 2, 4
POOL = NZ * NX * NC
ROWS = 256

BF = jnp.bfloat16
F32 = jnp.float32


def exchange_cores(value):
    return lax.ppermute(value, "c", [(0, 1), (1, 0)])


def shift_y(value, step):
    return lax.ppermute(value, "y", [(i, (i + step) % NY) for i in range(NY)])


def permute_xy(value, target):
    pairs = []
    for x in range(NX):
        for y in range(NY):
            to_x, to_y = target(x, y)
            pairs.append((x * NY + y, (to_x % NX) * NY + to_y % NY))
    return lax.ppermute(value, ("x", "y"), pairs)


def swap_zx(value):
    return lax.all_to_all(value, ("z", "x"), 0, 0, tiled=True)


def parts_of(value):
    high = lax.reduce_precision(value, 8, 7)
    rest = value - high
    middle = lax.reduce_precision(rest, 8, 7)
    low = rest - middle
    return [high.astype(BF), middle.astype(BF), low.astype(BF)]


def shift_x(value, step):
    return lax.ppermute(value, "x", [(i, (i + step) % NX) for i in range(NX)])


def swap_z(value):
    return lax.all_to_all(value, "z", 0, 0, tiled=True)


def hold(*values):
    return lax.optimization_barrier(values)


def positions(sel_index, doc_order):
    docs = jnp.arange(POOL, dtype=jnp.int32)
    slot_of_doc = jnp.sum(jnp.where(doc_order[:, None] == docs[None, :], docs[:, None], 0), axis=0)
    sel_doc = sel_index // DOC_LEN
    sel_tok = sel_index % DOC_LEN
    sel_slot = jnp.sum(
        jnp.where(sel_doc[:, None] == docs[None, :], slot_of_doc[None, :], 0), axis=1
    )
    sel_pos = sel_slot * DOC_LEN + sel_tok
    query_pos = DOC_LEN * POOL + docs
    row_pos = jnp.concatenate(
        [sel_pos.reshape(POOL, SEL_DEV), query_pos[:, None]], axis=1
    ).reshape(ROWS)
    return slot_of_doc, row_pos


def slices_kernel(place_ref, in_ref, out_ref, *rest):
    pieces, sems = rest[:4], rest[4]
    core = place_ref[0]
    y = place_ref[1]
    for go in (True, False):
        for step in range(4):
            base = lax.rem(y + step, NY) * 256

            def body(k, carry):
                far = k // NZ
                group = jnp.where(far == 0, core, 1 - core)
                start = pl.multiple_of((k - far * NZ) * 1024 + base + group * 128, 128)
                to = pl.multiple_of(k * 128, 128)
                first = pltpu.make_async_copy(
                    in_ref.at[:, pl.ds(start, 128)],
                    pieces[step].at[0:224, pl.ds(to, 128)],
                    sems.at[step, 0, k],
                )
                second = pltpu.make_async_copy(
                    out_ref.at[:, pl.ds(start, 128)],
                    pieces[step].at[224:336, pl.ds(to, 128)],
                    sems.at[step, 1, k],
                )
                if go:
                    first.start()
                    second.start()
                else:
                    first.wait()
                    second.wait()
                return carry

            lax.fori_loop(0, 16, body, 0)


def weight_slices(place, flat_in, w_out):
    hbm = pl.BlockSpec(memory_space=pl.ANY)
    return pl.pallas_call(
        slices_kernel,
        out_shape=tuple(jax.ShapeDtypeStruct((336, 2048), BF) for _ in range(4)),
        in_specs=[pl.BlockSpec(memory_space=pltpu.SMEM), hbm, hbm],
        out_specs=tuple(hbm for _ in range(4)),
        scratch_shapes=[pltpu.SemaphoreType.DMA((4, 2, 16))],
        cost_estimate=pl.CostEstimate(flops=0, bytes_accessed=11_000_000, transcendentals=0),
        name="weight_slices",
    )(place, flat_in, w_out)


NT = (((1,), (1,)), ((), ()))
TN = (((0,), (0,)), ((), ()))


def attend_kernel(
    place_ref, bias_ref, own_ref, other_ref, c0, c1, c2, c3, acc_ref, sent_ref, stat_ref
):
    core = place_ref[0]
    blocks = (c0, c1, c2, c3)
    stat_ref[...] = jnp.zeros_like(stat_ref)
    for rel in range(2):
        query_ref = own_ref if rel == 0 else other_ref
        group = core if rel == 0 else 1 - core
        key_at = pl.ds(pl.multiple_of(group * 128, 128), 128)
        value_at = pl.ds(pl.multiple_of(256 + group * 128, 128), 128)
        for half in range(2):
            lanes = slice(half * 256, half * 256 + 256)
            query = jnp.concatenate(
                [query_ref[half * 4 + i, 0:64, :] for i in range(4)], axis=0
            )
            scores = []
            top = jnp.full((1, 256), FLOOR, F32)
            for k in range(4):
                bias = bias_ref[k * 512 : k * 512 + 512, :]
                part = lax.dot_general(
                    blocks[k][:, key_at], query, NT, preferred_element_type=F32
                ) * (HEAD_DIM**-0.5) + jnp.concatenate([bias, bias], axis=1)
                scores.append(part)
                top = jnp.maximum(top, jnp.max(part, axis=0, keepdims=True))
            total = jnp.zeros((1, 256), F32)
            acc = jnp.zeros((128, 256), F32)
            for k in range(4):
                probs = jnp.exp(scores[k] - top)
                total = total + jnp.sum(probs, axis=0, keepdims=True)
                acc = acc + lax.dot_general(
                    blocks[k][:, value_at], probs.astype(BF), TN, preferred_element_type=F32
                )
            if rel == 0:
                acc_ref[:, lanes] = acc
            else:
                sent_ref[:, lanes] = acc.astype(BF)
            stat_ref[2 * rel : 2 * rel + 1, lanes] = top
            stat_ref[2 * rel + 1 : 2 * rel + 2, lanes] = total


def attend(place, bias, own, other, blocks):
    vmem = pl.BlockSpec(memory_space=pltpu.VMEM)
    return pl.pallas_call(
        attend_kernel,
        out_shape=(
            jax.ShapeDtypeStruct((128, 512), F32),
            jax.ShapeDtypeStruct((128, 512), BF),
            jax.ShapeDtypeStruct((8, 512), F32),
        ),
        in_specs=[pl.BlockSpec(memory_space=pltpu.SMEM)] + [vmem] * 7,
        out_specs=(vmem, vmem, vmem),
        compiler_params=pltpu.CompilerParams(vmem_limit_bytes=40 * 1024 * 1024),
        cost_estimate=pl.CostEstimate(
            flops=2 * 16 * 2 * 2048 * 128 * 64, bytes_accessed=6_000_000, transcendentals=2097152
        ),
        name="attend",
    )(place, bias, own, other, *blocks)


def merge_kernel(
    acc_ref, stat_ref, far_acc_ref, far_stat_ref, own_ref, key_ref, value_ref, bias_ref, out_ref
):
    query = jnp.concatenate([own_ref[i, 0:64, :] for i in range(8)], axis=0)
    bias = bias_ref[...]
    scores = lax.dot_general(key_ref[...], query, NT, preferred_element_type=F32) * (
        HEAD_DIM**-0.5
    ) + jnp.concatenate([bias] * 4, axis=1)
    near_top = stat_ref[0:1, :]
    far_top = far_stat_ref[2:3, :]
    top = jnp.maximum(jnp.maximum(near_top, far_top), jnp.max(scores, axis=0, keepdims=True))
    near = jnp.exp(near_top - top)
    far = jnp.exp(far_top - top)
    probs = jnp.exp(scores - top)
    total = (
        stat_ref[1:2, :] * near
        + far_stat_ref[3:4, :] * far
        + jnp.sum(probs, axis=0, keepdims=True)
    )
    acc = (
        acc_ref[...] * near
        + far_acc_ref[...].astype(F32) * far
        + lax.dot_general(value_ref[...], probs.astype(BF), TN, preferred_element_type=F32)
    )
    rows = acc.T.astype(BF)
    tops = []
    for value in (top, total):
        high = value.astype(BF)
        rest = value - high.astype(F32)
        middle = rest.astype(BF)
        low = (rest - middle.astype(F32)).astype(BF)
        tops += [high.astype(F32), middle.astype(F32), low.astype(F32)]
    stats = jnp.concatenate(tops + [jnp.zeros((10, 512), F32)], axis=0).astype(BF)
    for head in range(8):
        pair = head // 2
        out_ref[head, 0:64, :] = rows[head * 64 : head * 64 + 64, :]
        out_ref[head, 64:80, :] = stats[:, pair * 128 : pair * 128 + 128]


def merge(*operands):
    vmem = pl.BlockSpec(memory_space=pltpu.VMEM)
    return pl.pallas_call(
        merge_kernel,
        out_shape=jax.ShapeDtypeStruct((8, 80, 128), BF),
        in_specs=[vmem] * 8,
        out_specs=vmem,
        cost_estimate=pl.CostEstimate(
            flops=4 * 512 * 128 * 32, bytes_accessed=1_000_000, transcendentals=20000
        ),
        name="merge",
    )(*operands)


def shards(
    hidden_rows,
    cache_kv,
    sel_index,
    doc_order,
    attn_gain,
    w_query,
    w_keyval,
    w_output,
    ffn_gain,
    w_in,
    w_out,
):
    z, x, c, y = (lax.axis_index(name) for name in ("z", "x", "c", "y"))
    mine = (z * NX + x) * NC + c
    other = 1 - c

    def half(group):
        return jnp.concatenate(
            [
                lax.dynamic_slice_in_dim(w_query, group * 1024, 1024, 1),
                lax.dynamic_slice_in_dim(w_keyval[:, 0], group * 128, 128, 1),
                lax.dynamic_slice_in_dim(w_keyval[:, 1], group * 128, 128, 1),
            ],
            axis=1,
        )

    message = jnp.concatenate(
        [hidden_rows, jnp.broadcast_to(attn_gain[None, :], (16, 128))], axis=0
    )
    theirs = exchange_cores(message)
    weight_theirs = exchange_cores(half(other))

    cache = cache_kv.reshape(DOC_LEN, 512)
    right, left = shift_x(cache, 1), shift_x(cache, -1)
    across = shift_x(right, 1)

    weight = jnp.concatenate([half(c), weight_theirs], axis=0)
    inputs = jnp.concatenate([hidden_rows, theirs[:ROWS]], axis=1).astype(F32)
    gain = jnp.concatenate([attn_gain, theirs[ROWS]], axis=0).astype(F32)
    squares = jnp.sum(inputs * inputs, axis=1)
    scaled = (inputs * gain[None, :]).astype(BF)
    partial = jnp.dot(scaled, weight, preferred_element_type=F32).astype(BF)
    query_part = jnp.transpose(partial[:, :1024].reshape(4, 64, 8, 128), (2, 0, 1, 3))
    new_part = jnp.transpose(partial[:, 1024:].reshape(4, 8, 8, 2, 128), (1, 0, 3, 2, 4))
    square_parts = jnp.stack(parts_of(squares) + [jnp.zeros((ROWS,), BF)] * 5).reshape(8, 4, 64)
    square_parts = jnp.pad(jnp.transpose(square_parts, (1, 0, 2)), ((0, 0), (0, 0), (0, 64)))
    payload = jnp.concatenate(
        [
            query_part,
            new_part.reshape(8, 4, 16, 128),
            jnp.broadcast_to(square_parts[None], (8, 4, 8, 128)),
        ],
        axis=2,
    ).reshape(32, 88, 128)
    total = jnp.sum(swap_zx(payload).astype(F32), axis=0)
    square_sum = (total[80] + (total[81] + total[82]))[:64]
    factor = lax.rsqrt(square_sum / D + EPS)
    near = lax.dynamic_slice_in_dim(factor, z * 8, 8, 0)
    piece = jnp.concatenate(
        [
            total[:64] * factor[:, None],
            (total[64:80].reshape(2, 8, 128) * near[None, :, None]).reshape(16, 128),
        ],
        axis=0,
    ).astype(BF)

    place = jnp.stack([c, y]).astype(jnp.int32)
    flat_in = jnp.transpose(w_in, (1, 2, 0)).reshape(224, D)
    pieces = weight_slices(place, flat_in, w_out)
    slices = [pieces[0], shift_y(pieces[1], 1), None, shift_y(pieces[3], 3)]

    slot_of_doc, row_pos = positions(sel_index, doc_order)
    my_pos = lax.dynamic_slice_in_dim(row_pos, x * 64, 64, 0)
    my_pos = jnp.concatenate([my_pos, my_pos])[None, :]
    token = jnp.arange(8, dtype=jnp.int32)
    docs = jnp.arange(POOL, dtype=jnp.int32)
    key_pos = []
    for step in (0, 1, 3, 2):
        base = ((z * NX + (x - step) % NX) * NC + c) * 8
        name = (docs[:, None] * DOC_LEN + base + token[None, :]).reshape(DOC_LEN)
        at = (slot_of_doc[:, None] * DOC_LEN + base + token[None, :]).reshape(DOC_LEN)
        written = jnp.any(name[:, None] == sel_index[None, :], axis=1)
        key_pos.append(jnp.where(written, DOC_LEN * POOL * 2, at))
    bias = jnp.where(jnp.concatenate(key_pos)[:, None] <= my_pos, 0.0, NEG).astype(F32)
    new_pos = lax.dynamic_slice_in_dim(row_pos, z * 32, 32, 0)
    new_bias = jnp.where(new_pos[:, None] <= my_pos, 0.0, NEG).astype(F32)

    piece, right, left, across, wo, bias = hold(piece, right, left, across, w_output, bias)
    own = swap_z(jnp.broadcast_to(piece[None], (8, 80, 128)))
    wo_right, wo_left = shift_x(wo, 1), shift_x(wo, -1)
    wo_across = shift_x(wo_right, 1)
    others = exchange_cores(own)
    new = jnp.stack([own[:, 64:], others[:, 64:]])
    acc, acc_sent, stats = attend(place, bias, own, others, (cache, right, left, across))

    new_right, new_left = shift_x(new, 1), shift_x(new, -1)
    new_all = jnp.stack([new, new_right, shift_x(new_right, 1), new_left])
    new_here = lax.dynamic_index_in_dim(new_all[:, 0], (x - z // 2) % NX, 0, keepdims=False)
    new_here = lax.dynamic_slice_in_dim(new_here, (z % 2) * 4, 4, 0).reshape(4, 2, 8, 128)

    far_acc = exchange_cores(acc_sent)
    far_stats = exchange_cores(stats)
    payload = merge(
        acc,
        stats,
        far_acc,
        far_stats,
        own,
        new_here[:, 0].reshape(32, 128),
        new_here[:, 1].reshape(32, 128),
        new_bias,
    )
    payload, slices[1], slices[3], last = hold(payload, slices[1], slices[3], pieces[2])
    slices[2] = shift_y(last, 2)
    arrived = swap_z(payload).astype(F32)
    lane = (z % 2) * 64
    tops = arrived[:, 64] + (arrived[:, 65] + arrived[:, 66])
    sums = arrived[:, 67] + (arrived[:, 68] + arrived[:, 69])
    tops = lax.dynamic_slice_in_dim(tops, lane, 64, 1)
    sums = lax.dynamic_slice_in_dim(sums, lane, 64, 1)
    by = jnp.exp(tops - jnp.max(tops, axis=0, keepdims=True))
    norm = jnp.sum(sums * by, axis=0)
    summed = jnp.sum(arrived[:, :64] * by[:, :, None], axis=0)
    piece = (summed / norm[:, None]).astype(BF)
    piece, wo_right, wo_left, wo_across = hold(piece, wo_right, wo_left, wo_across)
    attended = swap_z(jnp.broadcast_to(piece[None], (8, 64, 128)))
    attended_theirs = exchange_cores(attended)

    def flat(value):
        return jnp.transpose(value, (1, 0, 2)).reshape(64, 1024)

    wo_all = jnp.concatenate([w_output, wo_right, wo_across, wo_left], axis=1)
    wo_own = lax.dynamic_slice_in_dim(wo_all, c * 1024, 1024, 0)
    wo_theirs = lax.dynamic_slice_in_dim(wo_all, other * 1024, 1024, 0)
    projected = jnp.dot(flat(attended), wo_own, preferred_element_type=F32)
    projected = projected + jnp.dot(flat(attended_theirs), wo_theirs, preferred_element_type=F32)
    chunks = jnp.transpose(projected.reshape(64, 4, 128), (1, 0, 2))
    early = jnp.concatenate(
        [
            lax.dynamic_slice_in_dim(hidden_rows, y * 64, 64, 0),
            jnp.broadcast_to(ffn_gain[None, :], (16, 128)),
        ],
        axis=0,
    )
    early = permute_xy(early, lambda a, b: (b, a))
    chunks, slices[2] = hold(chunks, slices[2])
    mid = early[:64].astype(F32) + lax.dynamic_index_in_dim(chunks, (x - y) % NX, 0, keepdims=False)
    chunks = chunks.astype(BF)
    for step in range(1, 4):
        sent = lax.dynamic_index_in_dim(chunks, (x - y - step) % NX, 0, keepdims=False)
        mid = mid + shift_y(sent, step).astype(F32)
    feature = (mid * early[64].astype(F32)[None, :]).astype(BF)
    square_parts = jnp.stack(parts_of(jnp.sum(mid * mid, axis=1)) + [jnp.zeros((64,), BF)] * 5)
    payload = jnp.concatenate([feature, jnp.pad(square_parts, ((0, 0), (0, 64)))], axis=0)
    arrived = swap_zx(jnp.broadcast_to(payload[None], (32, 72, 128)))
    arrived_theirs = exchange_cores(arrived)

    reordered = cache.reshape(POOL, 8, 512).at[doc_order].get(mode="promise_in_bounds")
    reordered = reordered.reshape(32, 2, 8, 512)
    stay = lax.dynamic_index_in_dim(reordered, c, 1, keepdims=False)
    leave = lax.dynamic_index_in_dim(reordered, other, 1, keepdims=False)
    come = exchange_cores(leave)
    lower = jnp.where(c == 0, stay, come)
    upper = jnp.where(c == 0, come, stay)
    cache_out = jnp.concatenate([lower, upper], axis=1)
    arrived, cache_out = hold(arrived, cache_out)
    slot_cache = swap_zx(cache_out)

    def features_of(block):
        return jnp.transpose(block[:, :64].reshape(NZ, ROWS, 128), (1, 0, 2)).reshape(ROWS, 1024)

    def squares_of(block):
        parts = jnp.sum(block[:, 64:67, :64].astype(F32), axis=1)
        return jnp.sum(parts.reshape(NZ, ROWS), axis=0)

    feature_own = features_of(arrived)
    feature_theirs = features_of(arrived_theirs)
    square_sum = squares_of(arrived) + squares_of(arrived_theirs)
    square_rows = jnp.stack(parts_of(square_sum) + [jnp.zeros((ROWS,), BF)] * 5)
    hidden = []
    for step in range(4):
        term = lax.dot_general(
            slices[step][:224, :1024], feature_own, NT, preferred_element_type=F32
        ) + lax.dot_general(
            slices[step][:224, 1024:], feature_theirs, NT, preferred_element_type=F32
        )
        hidden.append(term)
    both = hidden[0]
    for step in range(1, 4):
        sent = jnp.concatenate([hidden[step].astype(BF), square_rows], axis=0)
        got = shift_y(sent, -step).astype(F32)
        both = both + got[:224]
        square_sum = square_sum + (got[224] + (got[225] + got[226]))
    both = both * lax.rsqrt(square_sum / D + EPS)[None, :]
    act = (jax.nn.silu(both[:112]) * both[112:]).astype(BF)
    acts = [act] + [shift_y(act, step) for step in range(1, 4)]
    act_all = jnp.concatenate(acts, axis=0)
    out_all = jnp.concatenate([item[224:] for item in slices], axis=0)
    term_theirs = lax.dot_general(act_all, out_all[:, 1024:], TN, preferred_element_type=F32)
    got = exchange_cores(term_theirs.astype(BF))
    term = lax.dot_general(act_all, out_all[:, :1024], TN, preferred_element_type=F32)
    term = (term + got.astype(F32)).astype(BF)
    payload = jnp.transpose(term.reshape(ROWS, NZ, 128), (1, 0, 2)).reshape(32, 64, 128)
    payload, slot_cache = hold(payload, slot_cache)
    down = jnp.sum(swap_zx(payload).astype(F32), axis=0)
    result = permute_xy((mid + down).astype(BF), lambda a, b: (b, a))

    sel_key = jnp.where(row_pos // DOC_LEN == mine, row_pos % DOC_LEN, -1)
    sel_key = jnp.concatenate(
        [lax.dynamic_slice_in_dim(sel_key, ((x - k) % NX) * 64, 64, 0) for k in range(4)]
    )
    hits = sel_key[None, :] == jnp.arange(DOC_LEN, dtype=jnp.int32)[:, None]
    covered = jnp.any(hits, axis=1)
    new_flat = new_all.reshape(4, 2, 8, 2, 8, 128)
    new_flat = jnp.where(c == 0, new_flat, new_flat[:, ::-1])
    new_flat = jnp.transpose(new_flat, (0, 2, 4, 3, 1, 5)).reshape(ROWS, 512)
    placed = jnp.dot(hits.astype(BF), new_flat, preferred_element_type=F32).astype(BF)
    joined = jnp.where(covered[:, None], placed, slot_cache.reshape(DOC_LEN, 512))
    return (result, joined.reshape(DOC_LEN, 2, 256))


def solution(mesh):
    split = Mesh(mesh.devices.reshape(NZ, NX, NC, NY), ("z", "x", "c", "y"))
    pool = ("z", "x", "c")
    return jax.shard_map(
        shards,
        mesh=split,
        in_specs=(
            P(None, pool),
            P(None, pool, None, "y"),
            P(),
            P(),
            P(pool),
            P(pool, "y"),
            P(pool, None, "y"),
            P("y", pool),
            P(pool),
            P(None, None, ("z", "x", "c", "y")),
            P(("z", "x", "c", "y"), None),
        ),
        out_specs=(P("y", pool), P(pool, None, "y")),
        check_vma=False,
    )
```

```python
import functools

import jax
import jax.numpy as jnp
from jax import lax
from jax.experimental import pallas as pl
from jax.experimental.pallas import tpu as pltpu
from jax.sharding import Mesh
from jax.sharding import PartitionSpec as P

D = 8192
HEAD_DIM = 128
DOC_LEN = 512
SEL_DEV = 3
EPS = 1e-05
NEG = -1e30
FLOOR = -1e29
NZ, NX, NC, NY = 8, 4, 2, 4
POOL = NZ * NX * NC
ROWS = 256

BF = jnp.bfloat16
F32 = jnp.float32


def exchange_cores(value):
    return lax.ppermute(value, "c", [(0, 1), (1, 0)])


def shift_y(value, step):
    return lax.ppermute(value, "y", [(i, (i + step) % NY) for i in range(NY)])


def permute_xy(value, target):
    pairs = []
    for x in range(NX):
        for y in range(NY):
            to_x, to_y = target(x, y)
            pairs.append((x * NY + y, (to_x % NX) * NY + to_y % NY))
    return lax.ppermute(value, ("x", "y"), pairs)


def swap_zx(value):
    return lax.all_to_all(value, ("z", "x"), 0, 0, tiled=True)


def parts_of(value):
    high = lax.reduce_precision(value, 8, 7)
    rest = value - high
    middle = lax.reduce_precision(rest, 8, 7)
    low = rest - middle
    return [high.astype(BF), middle.astype(BF), low.astype(BF)]


def shift_x(value, step):
    return lax.ppermute(value, "x", [(i, (i + step) % NX) for i in range(NX)])


def swap_z(value):
    return lax.all_to_all(value, "z", 0, 0, tiled=True)


def hold(*values):
    return lax.optimization_barrier(values)


def positions(sel_index, doc_order):
    docs = jnp.arange(POOL, dtype=jnp.int32)
    slot_of_doc = jnp.sum(jnp.where(doc_order[:, None] == docs[None, :], docs[:, None], 0), axis=0)
    sel_doc = sel_index // DOC_LEN
    sel_tok = sel_index % DOC_LEN
    sel_slot = jnp.sum(
        jnp.where(sel_doc[:, None] == docs[None, :], slot_of_doc[None, :], 0), axis=1
    )
    sel_pos = sel_slot * DOC_LEN + sel_tok
    query_pos = DOC_LEN * POOL + docs
    row_pos = jnp.concatenate(
        [sel_pos.reshape(POOL, SEL_DEV), query_pos[:, None]], axis=1
    ).reshape(ROWS)
    return slot_of_doc, row_pos


def slices_kernel(place_ref, in_ref, out_ref, *pieces):
    core = place_ref[0]
    y = place_ref[1]
    for step in range(4):
        base = lax.rem(y + step, NY) * 256
        for rel in range(2):
            group = core if rel == 0 else 1 - core
            lanes = pl.ds(pl.multiple_of(base + group * 128, 128), 128)
            pieces[step][rel, 0:224, :] = in_ref[:, lanes]
            pieces[step][rel, 224:336, :] = out_ref[:, lanes]


def weight_slices(place, flat_in, w_out):
    return pl.pallas_call(
        slices_kernel,
        grid=(NZ,),
        out_shape=tuple(jax.ShapeDtypeStruct((2, 336, 1024), BF) for _ in range(4)),
        in_specs=[
            pl.BlockSpec(memory_space=pltpu.SMEM),
            pl.BlockSpec((224, 1024), lambda k: (0, k)),
            pl.BlockSpec((112, 1024), lambda k: (0, k)),
        ],
        out_specs=tuple(pl.BlockSpec((2, 336, 128), lambda k: (0, 0, k)) for _ in range(4)),
        cost_estimate=pl.CostEstimate(flops=0, bytes_accessed=11_000_000, transcendentals=0),
        name="weight_slices",
    )(place, flat_in, w_out)


NT = (((1,), (1,)), ((), ()))
TN = (((0,), (0,)), ((), ()))


def attend_kernel(
    place_ref, bias_ref, own_ref, other_ref, c0, c1, c2, c3, acc_ref, sent_ref, stat_ref
):
    core = place_ref[0]
    blocks = (c0, c1, c2, c3)
    stat_ref[...] = jnp.zeros_like(stat_ref)
    for rel in range(2):
        query_ref = own_ref if rel == 0 else other_ref
        group = core if rel == 0 else 1 - core
        key_at = pl.ds(pl.multiple_of(group * 128, 128), 128)
        value_at = pl.ds(pl.multiple_of(256 + group * 128, 128), 128)
        for half in range(2):
            lanes = slice(half * 256, half * 256 + 256)
            query = jnp.concatenate(
                [query_ref[half * 4 + i, 0:64, :] for i in range(4)], axis=0
            )
            scores = []
            top = jnp.full((1, 256), FLOOR, F32)
            for k in range(4):
                bias = bias_ref[k * 512 : k * 512 + 512, :]
                part = lax.dot_general(
                    blocks[k][:, key_at], query, NT, preferred_element_type=F32
                ) * (HEAD_DIM**-0.5) + jnp.concatenate([bias, bias], axis=1)
                scores.append(part)
                top = jnp.maximum(top, jnp.max(part, axis=0, keepdims=True))
            total = jnp.zeros((1, 256), F32)
            acc = jnp.zeros((128, 256), F32)
            for k in range(4):
                probs = jnp.exp(scores[k] - top)
                total = total + jnp.sum(probs, axis=0, keepdims=True)
                acc = acc + lax.dot_general(
                    blocks[k][:, value_at], probs.astype(BF), TN, preferred_element_type=F32
                )
            if rel == 0:
                acc_ref[:, lanes] = acc
            else:
                sent_ref[:, lanes] = acc.astype(BF)
            stat_ref[2 * rel : 2 * rel + 1, lanes] = top
            stat_ref[2 * rel + 1 : 2 * rel + 2, lanes] = total


def attend(place, bias, own, other, blocks):
    vmem = pl.BlockSpec(memory_space=pltpu.VMEM)
    return pl.pallas_call(
        attend_kernel,
        out_shape=(
            jax.ShapeDtypeStruct((128, 512), F32),
            jax.ShapeDtypeStruct((128, 512), BF),
            jax.ShapeDtypeStruct((8, 512), F32),
        ),
        in_specs=[pl.BlockSpec(memory_space=pltpu.SMEM)] + [vmem] * 7,
        out_specs=(vmem, vmem, vmem),
        compiler_params=pltpu.CompilerParams(vmem_limit_bytes=40 * 1024 * 1024),
        cost_estimate=pl.CostEstimate(
            flops=2 * 16 * 2 * 2048 * 128 * 64, bytes_accessed=6_000_000, transcendentals=2097152
        ),
        name="attend",
    )(place, bias, own, other, *blocks)


def split_rows(value):
    high = value.astype(BF).astype(F32)
    rest = value - high
    middle = rest.astype(BF).astype(F32)
    return [high, middle, rest - middle]


def merge_kernel(acc_ref, stat_ref, far_acc_ref, far_stat_ref, out_ref):
    near_top = stat_ref[0:1, :]
    far_top = far_stat_ref[2:3, :]
    top = jnp.maximum(near_top, far_top)
    near = jnp.exp(near_top - top)
    far = jnp.exp(far_top - top)
    total = stat_ref[1:2, :] * near + far_stat_ref[3:4, :] * far
    acc = acc_ref[...] * near + far_acc_ref[...].astype(F32) * far
    rows = acc.T.astype(BF)
    stats = split_rows(top) + split_rows(total) + [jnp.zeros((10, 512), F32)]
    stats = jnp.concatenate(stats, axis=0).astype(BF)
    for head in range(8):
        pair = head // 2
        out_ref[head, 0:64, :] = rows[head * 64 : head * 64 + 64, :]
        out_ref[head, 64:80, :] = stats[:, pair * 128 : pair * 128 + 128]


VMEM = pl.BlockSpec(memory_space=pltpu.VMEM)
SMEM = pl.BlockSpec(memory_space=pltpu.SMEM)


def merge(*operands):
    return pl.pallas_call(
        merge_kernel,
        out_shape=jax.ShapeDtypeStruct((8, 80, 128), BF),
        in_specs=[VMEM] * 4,
        out_specs=VMEM,
        cost_estimate=pl.CostEstimate(flops=500_000, bytes_accessed=1_000_000, transcendentals=0),
        name="merge",
    )(*operands)


def finish_kernel(
    place_ref, arrived_ref, own_ref, key_ref, value_ref, bias_ref, out_ref, column_ref, new_ref
):
    z = place_ref[0]
    query = own_ref[z, 0:64, :]
    query = jnp.concatenate([query, query], axis=0)
    scores = lax.dot_general(key_ref[...], query, NT, preferred_element_type=F32)
    scores = scores * (HEAD_DIM**-0.5) + bias_ref[...]
    tops = []
    sums = []
    for k in range(8):
        stat = arrived_ref[k, 64:80, :].astype(F32)
        tops.append(stat[0:1] + (stat[1:2] + stat[2:3]))
        sums.append(stat[3:4] + (stat[4:5] + stat[5:6]))
    tops = jnp.concatenate(tops, axis=0)
    sums = jnp.concatenate(sums, axis=0)
    top = jnp.maximum(
        jnp.max(tops, axis=0, keepdims=True), jnp.max(scores, axis=0, keepdims=True)
    )
    by = jnp.exp(tops - top)
    probs = jnp.exp(scores - top)
    norm = jnp.sum(sums * by, axis=0, keepdims=True) + jnp.sum(probs, axis=0, keepdims=True)
    column_ref[...] = jnp.concatenate([by, jnp.broadcast_to(norm, (8, 128))], axis=0).T
    new_ref[...] = lax.dot_general(
        probs.astype(BF), value_ref[...], TN, preferred_element_type=F32
    )
    mine = pl.ds(pl.multiple_of(lax.rem(z, 2) * 64, 64), 64)
    column = column_ref[mine, :]
    acc = new_ref[mine, :]
    for k in range(8):
        acc = acc + arrived_ref[k, 0:64, :].astype(F32) * column[:, k : k + 1]
    result = (acc / column[:, 8:9]).astype(BF)
    for k in range(8):
        out_ref[k] = result


def finish(*operands):
    return pl.pallas_call(
        finish_kernel,
        out_shape=jax.ShapeDtypeStruct((8, 64, 128), BF),
        in_specs=[SMEM] + [VMEM] * 5,
        out_specs=VMEM,
        scratch_shapes=[pltpu.VMEM((128, 16), F32), pltpu.VMEM((128, 128), F32)],
        cost_estimate=pl.CostEstimate(flops=20_000_000, bytes_accessed=800_000, transcendentals=0),
        name="finish",
    )(*operands)


def ffn_in_kernel(p0, p1, p2, p3, own_ref, far_ref, keep_ref, square_ref, s1, s2, s3, feature):
    pairs = [jnp.zeros((1, 128), F32), jnp.zeros((1, 128), F32)]
    for rel, ref in enumerate((own_ref, far_ref)):
        for z in range(NZ):
            for k in range(4):
                feature[rel, k * 64 : k * 64 + 64, z * 128 : z * 128 + 128] = ref[
                    z * 4 + k, 0:64, :
                ]
                stat = ref[z * 4 + k, 64:80, :].astype(F32)
                pairs[k // 2] = pairs[k // 2] + (stat[0:1] + (stat[1:2] + stat[2:3]))
    squares = jnp.concatenate(pairs, axis=1)
    square_ref[...] = jnp.broadcast_to(squares, (8, ROWS))
    rows = jnp.concatenate(split_rows(squares) + [jnp.zeros((13, ROWS), F32)], axis=0).astype(BF)
    for step, (piece, to) in enumerate(((p1, s1), (p2, s2), (p3, s3), (p0, keep_ref))):
        value = lax.dot_general(
            piece[0, 0:224, :], feature[0], NT, preferred_element_type=F32
        ) + lax.dot_general(piece[1, 0:224, :], feature[1], NT, preferred_element_type=F32)
        if step < 3:
            to[0:224, :] = value.astype(BF)
            to[224:240, :] = rows
        else:
            to[...] = value


def ffn_in(*operands):
    sent = jax.ShapeDtypeStruct((240, ROWS), BF)
    return pl.pallas_call(
        ffn_in_kernel,
        out_shape=(
            jax.ShapeDtypeStruct((224, ROWS), F32),
            jax.ShapeDtypeStruct((8, ROWS), F32),
            sent,
            sent,
            sent,
        ),
        in_specs=[VMEM] * 6,
        out_specs=(VMEM,) * 5,
        scratch_shapes=[pltpu.VMEM((2, ROWS, 1024), BF)],
        compiler_params=pltpu.CompilerParams(vmem_limit_bytes=40 * 1024 * 1024),
        cost_estimate=pl.CostEstimate(
            flops=2 * 896 * 2048 * 256, bytes_accessed=7_500_000, transcendentals=0
        ),
        name="ffn_in",
    )(*operands)


def ffn_out_kernel(p0, p1, p2, p3, a0, a1, a2, a3, sent_ref, keep_ref):
    act = jnp.concatenate([a0[...], a1[...], a2[...], a3[...]], axis=0)
    for rel in (1, 0):
        weight = jnp.concatenate([p[rel, 224:336, :] for p in (p0, p1, p2, p3)], axis=0)
        term = lax.dot_general(act, weight, TN, preferred_element_type=F32)
        for z in range(NZ):
            block = term[:, z * 128 : z * 128 + 128]
            if rel == 1:
                sent_ref[z] = block.astype(BF)
            else:
                keep_ref[z] = block


def ffn_out(*operands):
    return pl.pallas_call(
        ffn_out_kernel,
        out_shape=(
            jax.ShapeDtypeStruct((NZ, ROWS, 128), BF),
            jax.ShapeDtypeStruct((NZ, ROWS, 128), F32),
        ),
        in_specs=[VMEM] * 8,
        out_specs=(VMEM, VMEM),
        compiler_params=pltpu.CompilerParams(vmem_limit_bytes=40 * 1024 * 1024),
        cost_estimate=pl.CostEstimate(
            flops=2 * 448 * 2048 * 256, bytes_accessed=7_500_000, transcendentals=0
        ),
        name="ffn_out",
    )(*operands)


def shards(
    hidden_rows,
    cache_kv,
    sel_index,
    doc_order,
    attn_gain,
    w_query,
    w_keyval,
    w_output,
    ffn_gain,
    w_in,
    w_out,
):
    z, x, c, y = (lax.axis_index(name) for name in ("z", "x", "c", "y"))
    mine = (z * NX + x) * NC + c
    other = 1 - c

    def half(group):
        return jnp.concatenate(
            [
                lax.dynamic_slice_in_dim(w_query, group * 1024, 1024, 1),
                lax.dynamic_slice_in_dim(w_keyval[:, 0], group * 128, 128, 1),
                lax.dynamic_slice_in_dim(w_keyval[:, 1], group * 128, 128, 1),
            ],
            axis=1,
        )

    message = jnp.concatenate(
        [hidden_rows, jnp.broadcast_to(attn_gain[None, :], (16, 128))], axis=0
    )
    theirs = exchange_cores(message)
    weight_theirs = exchange_cores(half(other))

    weight = jnp.concatenate([half(c), weight_theirs], axis=0)
    inputs = jnp.concatenate([hidden_rows, theirs[:ROWS]], axis=1).astype(F32)
    gain = jnp.concatenate([attn_gain, theirs[ROWS]], axis=0).astype(F32)
    squares = jnp.sum(inputs * inputs, axis=1)
    scaled = (inputs * gain[None, :]).astype(BF)
    partial = jnp.dot(scaled, weight, preferred_element_type=F32).astype(BF)
    query_part = jnp.transpose(partial[:, :1024].reshape(4, 64, 8, 128), (2, 0, 1, 3))
    new_part = jnp.transpose(partial[:, 1024:].reshape(4, 8, 8, 2, 128), (1, 0, 3, 2, 4))
    square_parts = jnp.stack(parts_of(squares) + [jnp.zeros((ROWS,), BF)] * 5).reshape(8, 4, 64)
    square_parts = jnp.pad(jnp.transpose(square_parts, (1, 0, 2)), ((0, 0), (0, 0), (0, 64)))
    payload = jnp.concatenate(
        [
            query_part,
            new_part.reshape(8, 4, 16, 128),
            jnp.broadcast_to(square_parts[None], (8, 4, 8, 128)),
        ],
        axis=2,
    ).reshape(32, 88, 128)

    payload, cache = hold(payload, cache_kv.reshape(DOC_LEN, 512))
    right, left = shift_x(cache, 1), shift_x(cache, -1)
    across = shift_x(right, 1)
    total = jnp.sum(swap_zx(payload).astype(F32), axis=0)
    square_sum = (total[80] + (total[81] + total[82]))[:64]
    factor = lax.rsqrt(square_sum / D + EPS)
    near = lax.dynamic_slice_in_dim(factor, z * 8, 8, 0)
    piece = jnp.concatenate(
        [
            total[:64] * factor[:, None],
            (total[64:80].reshape(2, 8, 128) * near[None, :, None]).reshape(16, 128),
        ],
        axis=0,
    ).astype(BF)

    place = jnp.stack([c, y, z]).astype(jnp.int32)
    flat_in = jnp.transpose(w_in, (1, 2, 0)).reshape(224, D)
    pieces = weight_slices(place, flat_in, w_out)
    slices = [pieces[0], shift_y(pieces[1], 1), None, shift_y(pieces[3], 3)]

    slot_of_doc, row_pos = positions(sel_index, doc_order)
    my_pos = lax.dynamic_slice_in_dim(row_pos, x * 64, 64, 0)
    my_pos = jnp.concatenate([my_pos, my_pos])[None, :]
    token = jnp.arange(8, dtype=jnp.int32)
    docs = jnp.arange(POOL, dtype=jnp.int32)
    key_pos = []
    for step in (0, 1, 3, 2):
        base = ((z * NX + (x - step) % NX) * NC + c) * 8
        name = (docs[:, None] * DOC_LEN + base + token[None, :]).reshape(DOC_LEN)
        at = (slot_of_doc[:, None] * DOC_LEN + base + token[None, :]).reshape(DOC_LEN)
        written = jnp.any(name[:, None] == sel_index[None, :], axis=1)
        key_pos.append(jnp.where(written, DOC_LEN * POOL * 2, at))
    bias = jnp.where(jnp.concatenate(key_pos)[:, None] <= my_pos, 0.0, NEG).astype(F32)
    rel_pos = jnp.concatenate(
        [lax.dynamic_slice_in_dim(row_pos, ((x - k) % NX) * 64, 64, 0) for k in range(4)]
    )
    new_bias = jnp.where(rel_pos[:, None] <= my_pos, 0.0, NEG).astype(F32)

    piece, right, left, across, wo, bias, pieces = hold(
        piece, right, left, across, w_output, bias, pieces
    )
    own = swap_z(jnp.broadcast_to(piece[None], (8, 80, 128)))
    wo_right, wo_left = shift_x(wo, 1), shift_x(wo, -1)
    wo_across = shift_x(wo_right, 1)
    others = exchange_cores(own)
    new = jnp.stack([own[:, 64:], others[:, 64:]])
    acc, acc_sent, stats = attend(place, bias, own, others, (cache, right, left, across))

    new_right, new_left = shift_x(new, 1), shift_x(new, -1)
    new_all = jnp.stack([new, new_right, shift_x(new_right, 1), new_left])
    new_own = jnp.transpose(new_all[:, 0].reshape(4, 8, 2, 8, 128), (2, 0, 1, 3, 4))
    new_own = new_own.reshape(2, ROWS, 128)

    far_acc = exchange_cores(acc_sent)
    far_stats = exchange_cores(stats)
    payload = merge(acc, stats, far_acc, far_stats)
    payload, slices[1], slices[3], last = hold(payload, slices[1], slices[3], pieces[2])
    slices[2] = shift_y(last, 2)
    arrived = swap_z(payload)
    piece = finish(place[2:], arrived, own, new_own[0], new_own[1], new_bias)
    piece, wo_right, wo_left, wo_across = hold(piece, wo_right, wo_left, wo_across)
    attended = swap_z(piece)
    attended_theirs = exchange_cores(attended)

    def flat(value):
        return jnp.transpose(value, (1, 0, 2)).reshape(64, 1024)

    wo_all = jnp.concatenate([w_output, wo_right, wo_across, wo_left], axis=1)
    wo_own = lax.dynamic_slice_in_dim(wo_all, c * 1024, 1024, 0)
    wo_theirs = lax.dynamic_slice_in_dim(wo_all, other * 1024, 1024, 0)
    projected = jnp.dot(flat(attended), wo_own, preferred_element_type=F32)
    projected = projected + jnp.dot(flat(attended_theirs), wo_theirs, preferred_element_type=F32)
    chunks = jnp.transpose(projected.reshape(64, 4, 128), (1, 0, 2))
    early = jnp.concatenate(
        [
            lax.dynamic_slice_in_dim(hidden_rows, y * 64, 64, 0),
            jnp.broadcast_to(ffn_gain[None, :], (16, 128)),
        ],
        axis=0,
    )
    early = permute_xy(early, lambda a, b: (b, a))
    chunks, slices[2] = hold(chunks, slices[2])
    mid = early[:64].astype(F32) + lax.dynamic_index_in_dim(chunks, (x - y) % NX, 0, keepdims=False)
    chunks = chunks.astype(BF)
    for step in range(1, 4):
        sent = lax.dynamic_index_in_dim(chunks, (x - y - step) % NX, 0, keepdims=False)
        mid = mid + shift_y(sent, step).astype(F32)
    feature = (mid * early[64].astype(F32)[None, :]).astype(BF)
    square_parts = jnp.stack(parts_of(jnp.sum(mid * mid, axis=1)) + [jnp.zeros((64,), BF)] * 13)
    empty = jnp.zeros_like(square_parts)
    square_parts = jnp.where(
        x % 2 == 0,
        jnp.concatenate([square_parts, empty], axis=1),
        jnp.concatenate([empty, square_parts], axis=1),
    )
    payload = jnp.concatenate([feature, square_parts], axis=0)
    arrived = swap_zx(jnp.broadcast_to(payload[None], (32, 80, 128)))
    arrived_theirs = exchange_cores(arrived)

    reordered = cache.reshape(POOL, 8, 512).at[doc_order].get(mode="promise_in_bounds")
    reordered = reordered.reshape(32, 2, 8, 512)
    stay = lax.dynamic_index_in_dim(reordered, c, 1, keepdims=False)
    leave = lax.dynamic_index_in_dim(reordered, other, 1, keepdims=False)
    come = exchange_cores(leave)
    lower = jnp.where(c == 0, stay, come)
    upper = jnp.where(c == 0, come, stay)
    cache_out = jnp.concatenate([lower, upper], axis=1)
    arrived, cache_out = hold(arrived, cache_out)
    slot_cache = swap_zx(cache_out)

    both, squares, *sent = ffn_in(*slices, arrived, arrived_theirs)
    square_sum = squares[0]
    for step in range(1, 4):
        got = shift_y(sent[step - 1], -step).astype(F32)
        both = both + got[:224]
        square_sum = square_sum + (got[224] + (got[225] + got[226]))
    both = both * lax.rsqrt(square_sum / D + EPS)[None, :]
    act = (jax.nn.silu(both[:112]) * both[112:]).astype(BF)
    acts = [act] + [shift_y(act, step) for step in range(1, 4)]
    sent, keep = ffn_out(*slices, *acts)
    payload = (keep + exchange_cores(sent).astype(F32)).astype(BF).reshape(32, 64, 128)
    payload, slot_cache = hold(payload, slot_cache)
    down = jnp.sum(swap_zx(payload).astype(F32), axis=0)

    sel_key = jnp.where(row_pos // DOC_LEN == mine, row_pos % DOC_LEN, -1)
    sel_key = jnp.concatenate(
        [lax.dynamic_slice_in_dim(sel_key, ((x - k) % NX) * 64, 64, 0) for k in range(4)]
    )
    hits = sel_key[None, :] == jnp.arange(DOC_LEN, dtype=jnp.int32)[:, None]
    covered = jnp.any(hits, axis=1)
    new_flat = new_all.reshape(4, 2, 8, 2, 8, 128)
    new_flat = jnp.where(c == 0, new_flat, new_flat[:, ::-1])
    new_flat = jnp.transpose(new_flat, (0, 2, 4, 3, 1, 5)).reshape(ROWS, 512)
    placed = jnp.dot(hits.astype(BF), new_flat, preferred_element_type=F32).astype(BF)
    joined = jnp.where(covered[:, None], placed, slot_cache.reshape(DOC_LEN, 512))
    joined = joined.reshape(DOC_LEN, 2, 256)
    down, joined = hold(down, joined)
    result = permute_xy((mid + down).astype(BF), lambda a, b: (b, a))
    return (result, joined)


def solution(mesh):
    split = Mesh(mesh.devices.reshape(NZ, NX, NC, NY), ("z", "x", "c", "y"))
    pool = ("z", "x", "c")
    return jax.shard_map(
        shards,
        mesh=split,
        in_specs=(
            P(None, pool),
            P(None, pool, None, "y"),
            P(),
            P(),
            P(pool),
            P(pool, "y"),
            P(pool, None, "y"),
            P("y", pool),
            P(pool),
            P(None, None, ("z", "x", "c", "y")),
            P(("z", "x", "c", "y"), None),
        ),
        out_specs=(P("y", pool), P(pool, None, "y")),
        check_vma=False,
    )
```

```python
import functools

import jax
import jax.numpy as jnp
from jax import lax
from jax.experimental import pallas as pl
from jax.experimental.pallas import tpu as pltpu
from jax.sharding import Mesh
from jax.sharding import PartitionSpec as P

D = 8192
HEAD_DIM = 128
DOC_LEN = 512
SEL_DEV = 3
EPS = 1e-05
NEG = -1e30
FLOOR = -1e29
NZ, NX, NC, NY = 8, 4, 2, 4
POOL = NZ * NX * NC
ROWS = 256

BF = jnp.bfloat16
F32 = jnp.float32


def exchange_cores(value):
    return lax.ppermute(value, "c", [(0, 1), (1, 0)])


def shift_y(value, step):
    return lax.ppermute(value, "y", [(i, (i + step) % NY) for i in range(NY)])


def permute_xy(value, target):
    pairs = []
    for x in range(NX):
        for y in range(NY):
            to_x, to_y = target(x, y)
            pairs.append((x * NY + y, (to_x % NX) * NY + to_y % NY))
    return lax.ppermute(value, ("x", "y"), pairs)


def swap_zx(value):
    return lax.all_to_all(value, ("z", "x"), 0, 0, tiled=True)


def parts_of(value):
    high = lax.reduce_precision(value, 8, 7)
    rest = value - high
    middle = lax.reduce_precision(rest, 8, 7)
    low = rest - middle
    return [high.astype(BF), middle.astype(BF), low.astype(BF)]


def shift_x(value, step):
    return lax.ppermute(value, "x", [(i, (i + step) % NX) for i in range(NX)])


def swap_z(value):
    return lax.all_to_all(value, "z", 0, 0, tiled=True)


def hold(*values):
    return lax.optimization_barrier(values)


def positions(sel_index, doc_order):
    docs = jnp.arange(POOL, dtype=jnp.int32)
    slot_of_doc = jnp.sum(jnp.where(doc_order[:, None] == docs[None, :], docs[:, None], 0), axis=0)
    sel_doc = sel_index // DOC_LEN
    sel_tok = sel_index % DOC_LEN
    sel_slot = jnp.sum(
        jnp.where(sel_doc[:, None] == docs[None, :], slot_of_doc[None, :], 0), axis=1
    )
    sel_pos = sel_slot * DOC_LEN + sel_tok
    query_pos = DOC_LEN * POOL + docs
    row_pos = jnp.concatenate(
        [sel_pos.reshape(POOL, SEL_DEV), query_pos[:, None]], axis=1
    ).reshape(ROWS)
    return slot_of_doc, row_pos


def slices_kernel(place_ref, in_ref, out_ref, *pieces):
    core = place_ref[0]
    y = place_ref[1]
    for step in range(4):
        base = lax.rem(y + step, NY) * 256
        for rel in range(2):
            group = core if rel == 0 else 1 - core
            lanes = pl.ds(pl.multiple_of(base + group * 128, 128), 128)
            pieces[step][0, rel, 0:224, :] = in_ref[:, lanes]
            pieces[step][0, rel, 224:336, :] = out_ref[:, lanes]


def weight_slices(place, flat_in, w_out):
    return pl.pallas_call(
        slices_kernel,
        grid=(NZ,),
        out_shape=tuple(jax.ShapeDtypeStruct((NZ, 2, 336, 128), BF) for _ in range(4)),
        in_specs=[
            pl.BlockSpec(memory_space=pltpu.SMEM),
            pl.BlockSpec((224, 1024), lambda k: (0, k)),
            pl.BlockSpec((112, 1024), lambda k: (0, k)),
        ],
        out_specs=tuple(pl.BlockSpec((1, 2, 336, 128), lambda k: (k, 0, 0, 0)) for _ in range(4)),
        compiler_params=pltpu.CompilerParams(vmem_limit_bytes=8 * 1024 * 1024),
        cost_estimate=pl.CostEstimate(flops=0, bytes_accessed=11_000_000, transcendentals=0),
        name="weight_slices",
    )(place, flat_in, w_out)


NT = (((1,), (1,)), ((), ()))
TN = (((0,), (0,)), ((), ()))


def split_rows(value):
    high = value.astype(BF).astype(F32)
    rest = value - high
    middle = rest.astype(BF).astype(F32)
    return [high, middle, rest - middle]


def attend_kernel(
    place_ref, bias_ref, own_ref, other_ref, c0, c1, c2, c3, acc_ref, sent_ref, stat_ref
):
    core = place_ref[0]
    blocks = (c0, c1, c2, c3)
    for rel in range(2):
        query_ref = own_ref if rel == 0 else other_ref
        group = core if rel == 0 else 1 - core
        key_at = pl.ds(pl.multiple_of(group * 128, 128), 128)
        value_at = pl.ds(pl.multiple_of(256 + group * 128, 128), 128)
        for half in range(2):
            lanes = slice(half * 256, half * 256 + 256)
            query = jnp.concatenate(
                [query_ref[half * 4 + i, 0:64, :] for i in range(4)], axis=0
            )
            scores = []
            top = jnp.full((1, 256), FLOOR, F32)
            for k in range(4):
                bias = bias_ref[k * 512 : k * 512 + 512, :].astype(F32)
                part = lax.dot_general(
                    blocks[k][:, key_at], query, NT, preferred_element_type=F32
                ) * (HEAD_DIM**-0.5) + jnp.concatenate([bias, bias], axis=1)
                scores.append(part)
                top = jnp.maximum(top, jnp.max(part, axis=0, keepdims=True))
            total = jnp.zeros((1, 256), F32)
            acc = jnp.zeros((128, 256), F32)
            for k in range(4):
                probs = jnp.exp(scores[k] - top)
                total = total + jnp.sum(probs, axis=0, keepdims=True)
                acc = acc + lax.dot_general(
                    blocks[k][:, value_at], probs.astype(BF), TN, preferred_element_type=F32
                )
            if rel == 0:
                acc_ref[:, lanes] = acc
                stat_ref[0:1, lanes] = top
                stat_ref[1:2, lanes] = total
            else:
                stats = split_rows(top) + split_rows(total) + [jnp.zeros((10, 256), F32)]
                sent_ref[0:128, lanes] = acc.astype(BF)
                sent_ref[128:144, lanes] = jnp.concatenate(stats, axis=0).astype(BF)


def attend(place, bias, own, other, blocks):
    vmem = pl.BlockSpec(memory_space=pltpu.VMEM)
    return pl.pallas_call(
        attend_kernel,
        out_shape=(
            jax.ShapeDtypeStruct((128, 512), F32),
            jax.ShapeDtypeStruct((144, 512), BF),
            jax.ShapeDtypeStruct((8, 512), F32),
        ),
        in_specs=[pl.BlockSpec(memory_space=pltpu.SMEM)] + [vmem] * 7,
        out_specs=(vmem, vmem, vmem),
        compiler_params=pltpu.CompilerParams(vmem_limit_bytes=16 * 1024 * 1024),
        cost_estimate=pl.CostEstimate(
            flops=2 * 16 * 2 * 2048 * 128 * 64, bytes_accessed=6_000_000, transcendentals=2097152
        ),
        name="attend",
    )(place, bias, own, other, *blocks)


def merge_kernel(acc_ref, stat_ref, far_ref, out_ref):
    near_top = stat_ref[0:1, :]
    stat = far_ref[128:144, :].astype(F32)
    far_top = stat[0:1] + (stat[1:2] + stat[2:3])
    far_total = stat[3:4] + (stat[4:5] + stat[5:6])
    top = jnp.maximum(near_top, far_top)
    near = jnp.exp(near_top - top)
    far = jnp.exp(far_top - top)
    total = stat_ref[1:2, :] * near + far_total * far
    acc = acc_ref[...] * near + far_ref[0:128, :].astype(F32) * far
    rows = acc.T.astype(BF)
    stats = split_rows(top) + split_rows(total) + [jnp.zeros((10, 512), F32)]
    stats = jnp.concatenate(stats, axis=0).astype(BF)
    for head in range(8):
        pair = head // 2
        out_ref[head, 0:64, :] = rows[head * 64 : head * 64 + 64, :]
        out_ref[head, 64:80, :] = stats[:, pair * 128 : pair * 128 + 128]


VMEM = pl.BlockSpec(memory_space=pltpu.VMEM)
SMEM = pl.BlockSpec(memory_space=pltpu.SMEM)


def merge(*operands):
    return pl.pallas_call(
        merge_kernel,
        out_shape=jax.ShapeDtypeStruct((8, 80, 128), BF),
        in_specs=[VMEM] * 3,
        out_specs=VMEM,
        cost_estimate=pl.CostEstimate(flops=500_000, bytes_accessed=1_000_000, transcendentals=0),
        compiler_params=pltpu.CompilerParams(vmem_limit_bytes=6 * 1024 * 1024),
        name="merge",
    )(*operands)


def finish_kernel(
    place_ref, arrived_ref, own_ref, bias_ref, out_ref, column_ref, new_ref
):
    z = place_ref[0]
    keys = jnp.concatenate([own_ref[k, 64:96, :] for k in range(8)], axis=0)
    values = jnp.concatenate([own_ref[k, 96:128, :] for k in range(8)], axis=0)
    query = own_ref[z, 0:64, :]
    query = jnp.concatenate([query, query], axis=0)
    scores = lax.dot_general(keys, query, NT, preferred_element_type=F32)
    scores = scores * (HEAD_DIM**-0.5) + bias_ref[...].astype(F32)
    tops = []
    sums = []
    for k in range(8):
        stat = arrived_ref[k, 64:80, :].astype(F32)
        tops.append(stat[0:1] + (stat[1:2] + stat[2:3]))
        sums.append(stat[3:4] + (stat[4:5] + stat[5:6]))
    tops = jnp.concatenate(tops, axis=0)
    sums = jnp.concatenate(sums, axis=0)
    top = jnp.maximum(
        jnp.max(tops, axis=0, keepdims=True), jnp.max(scores, axis=0, keepdims=True)
    )
    by = jnp.exp(tops - top)
    probs = jnp.exp(scores - top)
    norm = jnp.sum(sums * by, axis=0, keepdims=True) + jnp.sum(probs, axis=0, keepdims=True)
    column_ref[...] = jnp.concatenate([by, jnp.broadcast_to(norm, (8, 128))], axis=0).T
    new_ref[...] = lax.dot_general(
        probs.astype(BF), values, TN, preferred_element_type=F32
    )
    mine = pl.ds(pl.multiple_of(lax.rem(z, 2) * 64, 64), 64)
    column = column_ref[mine, :]
    acc = new_ref[mine, :]
    for k in range(8):
        acc = acc + arrived_ref[k, 0:64, :].astype(F32) * column[:, k : k + 1]
    result = (acc / column[:, 8:9]).astype(BF)
    for k in range(8):
        out_ref[k] = result


def finish(*operands):
    return pl.pallas_call(
        finish_kernel,
        out_shape=jax.ShapeDtypeStruct((8, 64, 128), BF),
        in_specs=[SMEM] + [VMEM] * 3,
        out_specs=VMEM,
        scratch_shapes=[pltpu.VMEM((128, 16), F32), pltpu.VMEM((128, 128), F32)],
        cost_estimate=pl.CostEstimate(flops=20_000_000, bytes_accessed=800_000, transcendentals=0),
        compiler_params=pltpu.CompilerParams(vmem_limit_bytes=6 * 1024 * 1024),
        name="finish",
    )(*operands)


def project_kernel(place_ref, own_ref, far_ref, w0, w1, w2, w3, out_ref):
    core = place_ref[0]
    for k, weight_ref in enumerate((w0, w1, w2, w3)):
        value = jnp.zeros((64, 128), F32)
        for rel, ref in enumerate((own_ref, far_ref)):
            group = core if rel == 0 else 1 - core
            at = pl.ds(pl.multiple_of(group * 1024, 1024), 1024)
            rows = jnp.concatenate([ref[i] for i in range(8)], axis=1)
            value = value + jnp.dot(rows, weight_ref[at, :], preferred_element_type=F32)
        out_ref[k] = value


def project(*operands):
    return pl.pallas_call(
        project_kernel,
        out_shape=jax.ShapeDtypeStruct((NX, 64, 128), F32),
        in_specs=[SMEM] + [VMEM] * 6,
        out_specs=VMEM,
        compiler_params=pltpu.CompilerParams(vmem_limit_bytes=8 * 1024 * 1024),
        cost_estimate=pl.CostEstimate(
            flops=2 * 64 * 2048 * 512, bytes_accessed=2_500_000, transcendentals=0
        ),
        name="project",
    )(*operands)


def ffn_in_kernel(p0, p1, p2, p3, own_ref, far_ref, keep_ref, square_ref, s1, s2, s3, feature):
    pairs = [jnp.zeros((1, 128), F32), jnp.zeros((1, 128), F32)]
    for rel, ref in enumerate((own_ref, far_ref)):
        for z in range(NZ):
            for k in range(4):
                feature[rel, k * 64 : k * 64 + 64, z * 128 : z * 128 + 128] = ref[
                    z * 4 + k, 0:64, :
                ]
                stat = ref[z * 4 + k, 64:80, :].astype(F32)
                pairs[k // 2] = pairs[k // 2] + (stat[0:1] + (stat[1:2] + stat[2:3]))
    squares = jnp.concatenate(pairs, axis=1)
    square_ref[...] = jnp.broadcast_to(squares, (8, ROWS))
    rows = jnp.concatenate(split_rows(squares) + [jnp.zeros((13, ROWS), F32)], axis=0).astype(BF)
    for step, (piece, to) in enumerate(((p1, s1), (p2, s2), (p3, s3), (p0, keep_ref))):
        value = jnp.zeros((224, ROWS), F32)
        for rel in range(2):
            weight = jnp.concatenate([piece[z, rel, 0:224, :] for z in range(NZ)], axis=1)
            value = value + lax.dot_general(weight, feature[rel], NT, preferred_element_type=F32)
        if step < 3:
            to[0:224, :] = value.astype(BF)
            to[224:240, :] = rows
        else:
            to[...] = value


def ffn_in(*operands):
    sent = jax.ShapeDtypeStruct((240, ROWS), BF)
    return pl.pallas_call(
        ffn_in_kernel,
        out_shape=(
            jax.ShapeDtypeStruct((224, ROWS), F32),
            jax.ShapeDtypeStruct((8, ROWS), F32),
            sent,
            sent,
            sent,
        ),
        in_specs=[VMEM] * 6,
        out_specs=(VMEM,) * 5,
        scratch_shapes=[pltpu.VMEM((2, ROWS, 1024), BF)],
        compiler_params=pltpu.CompilerParams(vmem_limit_bytes=16 * 1024 * 1024),
        cost_estimate=pl.CostEstimate(
            flops=2 * 896 * 2048 * 256, bytes_accessed=7_500_000, transcendentals=0
        ),
        name="ffn_in",
    )(*operands)


def act_kernel(both_ref, square_ref, r1, r2, r3, out_ref):
    both = both_ref[...]
    squares = square_ref[0:1, :]
    for ref in (r1, r2, r3):
        both = both + ref[0:224, :].astype(F32)
        stat = ref[224:240, :].astype(F32)
        squares = squares + (stat[0:1] + (stat[1:2] + stat[2:3]))
    both = both * lax.rsqrt(squares / D + EPS)
    gate = both[0:112]
    out_ref[...] = (gate / (1.0 + jnp.exp(-gate)) * both[112:224]).astype(BF)


def act_of(*operands):
    return pl.pallas_call(
        act_kernel,
        out_shape=jax.ShapeDtypeStruct((112, ROWS), BF),
        in_specs=[VMEM] * 5,
        out_specs=VMEM,
        cost_estimate=pl.CostEstimate(flops=500_000, bytes_accessed=700_000, transcendentals=0),
        compiler_params=pltpu.CompilerParams(vmem_limit_bytes=6 * 1024 * 1024),
        name="act",
    )(*operands)


def down_kernel(rel, p0, p1, p2, p3, a0, a1, a2, a3, *refs):
    act = jnp.concatenate([a0[...], a1[...], a2[...], a3[...]], axis=0)
    weight = jnp.concatenate(
        [
            jnp.concatenate([p[z, rel, 224:336, :] for z in range(NZ)], axis=1)
            for p in (p0, p1, p2, p3)
        ],
        axis=0,
    )
    term = lax.dot_general(act, weight, TN, preferred_element_type=F32)
    for z in range(NZ):
        block = term[:, z * 128 : z * 128 + 128]
        if rel == 1:
            refs[-1][z] = block.astype(BF)
        else:
            block = (block + refs[0][z].astype(F32)).astype(BF)
            for k in range(NX):
                refs[-1][z * NX + k, 0:64, :] = block[k * 64 : k * 64 + 64, :]
                refs[-1][z * NX + k, 64:128, :] = refs[1][z * NX + k]


def down(rel, *operands):
    return pl.pallas_call(
        functools.partial(down_kernel, rel),
        out_shape=jax.ShapeDtypeStruct((NZ, ROWS, 128) if rel else (32, 128, 128), BF),
        in_specs=[VMEM] * len(operands),
        out_specs=VMEM,
        compiler_params=pltpu.CompilerParams(vmem_limit_bytes=16 * 1024 * 1024),
        cost_estimate=pl.CostEstimate(
            flops=448 * 2048 * 256, bytes_accessed=4_000_000, transcendentals=0
        ),
        name="down",
    )(*operands)


def shards(
    hidden_rows,
    cache_kv,
    sel_index,
    doc_order,
    attn_gain,
    w_query,
    w_keyval,
    w_output,
    ffn_gain,
    w_in,
    w_out,
):
    z, x, c, y = (lax.axis_index(name) for name in ("z", "x", "c", "y"))
    mine = (z * NX + x) * NC + c
    other = 1 - c

    def half(group):
        return jnp.concatenate(
            [
                lax.dynamic_slice_in_dim(w_query, group * 1024, 1024, 1),
                lax.dynamic_slice_in_dim(w_keyval[:, 0], group * 128, 128, 1),
                lax.dynamic_slice_in_dim(w_keyval[:, 1], group * 128, 128, 1),
            ],
            axis=1,
        )

    message = jnp.concatenate(
        [hidden_rows, jnp.broadcast_to(attn_gain[None, :], (16, 128))], axis=0
    )
    theirs = exchange_cores(message)
    weight_theirs = exchange_cores(half(other))

    theirs, raw = hold(theirs, cache_kv)
    cache = raw.reshape(DOC_LEN, 512)

    weight = jnp.concatenate([half(c), weight_theirs], axis=0)
    inputs = jnp.concatenate([hidden_rows, theirs[:ROWS]], axis=1).astype(F32)
    gain = jnp.concatenate([attn_gain, theirs[ROWS]], axis=0).astype(F32)
    squares = jnp.sum(inputs * inputs, axis=1)
    scaled = (inputs * gain[None, :]).astype(BF)
    partial = jnp.dot(scaled, weight, preferred_element_type=F32).astype(BF)
    query_part = jnp.transpose(partial[:, :1024].reshape(4, 64, 8, 128), (2, 0, 1, 3))
    new_part = jnp.transpose(partial[:, 1024:].reshape(8, 32, 2, 128), (0, 2, 1, 3))
    square_parts = jnp.stack(parts_of(squares) + [jnp.zeros((ROWS,), BF)] * 5)
    by_x = jnp.transpose(square_parts.reshape(8, 4, 64), (1, 0, 2))
    by_z = jnp.transpose(square_parts.reshape(8, 8, 32), (1, 0, 2))
    square_parts = jnp.concatenate(
        [
            jnp.broadcast_to(by_x[None], (8, 4, 8, 64)),
            jnp.broadcast_to(by_z[:, None], (8, 4, 8, 32)),
            jnp.zeros((8, 4, 8, 32), BF),
        ],
        axis=3,
    )
    new_part = jnp.broadcast_to(new_part.reshape(8, 1, 64, 128), (8, 4, 64, 128))
    payload = jnp.concatenate([query_part, new_part, square_parts], axis=2).reshape(32, 136, 128)

    early = jnp.concatenate(
        [
            lax.dynamic_slice_in_dim(hidden_rows, y * 64, 64, 0),
            jnp.broadcast_to(ffn_gain[None, :], (16, 128)),
        ],
        axis=0,
    )
    payload, cache, sel_index, doc_order, early = hold(
        payload, cache, sel_index, doc_order, early
    )
    reordered = cache.reshape(POOL, 8, 512).at[doc_order].get(mode="promise_in_bounds")
    reordered = reordered.reshape(32, 2, 8, 512)
    stay = lax.dynamic_index_in_dim(reordered, c, 1, keepdims=False)
    leave = lax.dynamic_index_in_dim(reordered, other, 1, keepdims=False)
    come, w_in, w_out, early = hold(exchange_cores(leave), w_in, w_out, early)
    early = permute_xy(early, lambda a, b: (b, a))
    right, left, across = shift_x(cache, 1), shift_x(cache, -1), shift_x(cache, 2)
    arrived, right, left, across = hold(swap_zx(payload), right, left, across)
    total = jnp.sum(arrived.astype(F32), axis=0)
    square_sum = total[128] + (total[129] + total[130])
    factor = lax.rsqrt(square_sum / D + EPS)
    new = total[64:128].reshape(2, 32, 128) * factor[None, 64:96, None]
    piece = jnp.concatenate(
        [total[:64] * factor[:64, None], new.reshape(64, 128)], axis=0
    ).astype(BF)

    place = jnp.stack([c, y, z]).astype(jnp.int32)
    flat_in = jnp.transpose(w_in, (1, 2, 0)).reshape(224, D)
    pieces = weight_slices(place, flat_in, w_out)
    slices = [pieces[0], shift_y(pieces[1], 1), None, shift_y(pieces[3], 3)]

    slot_of_doc, row_pos = positions(sel_index, doc_order)
    my_pos = lax.dynamic_slice_in_dim(row_pos, x * 64, 64, 0)
    my_pos = jnp.concatenate([my_pos, my_pos])[None, :]
    token = jnp.arange(8, dtype=jnp.int32)
    docs = jnp.arange(POOL, dtype=jnp.int32)
    key_pos = []
    for step in (0, 1, 3, 2):
        base = ((z * NX + (x - step) % NX) * NC + c) * 8
        name = (docs[:, None] * DOC_LEN + base + token[None, :]).reshape(DOC_LEN)
        at = (slot_of_doc[:, None] * DOC_LEN + base + token[None, :]).reshape(DOC_LEN)
        written = jnp.any(name[:, None] == sel_index[None, :], axis=1)
        key_pos.append(jnp.where(written, DOC_LEN * POOL * 2, at))
    bias = jnp.where(jnp.concatenate(key_pos)[:, None] <= my_pos, 0.0, NEG).astype(BF)
    new_bias = jnp.where(row_pos[:, None] <= my_pos, 0.0, NEG).astype(BF)

    piece, bias, new_bias, pieces, w_output = hold(piece, bias, new_bias, pieces, w_output)
    own = swap_z(jnp.broadcast_to(piece[None], (8, 128, 128)))
    wo_right, wo_left = shift_x(w_output, 1), shift_x(w_output, -1)
    others = exchange_cores(own)
    acc, acc_sent, stats = attend(place, bias, own, others, (cache, right, left, across))

    payload = merge(acc, stats, exchange_cores(acc_sent))
    payload, w_output, wo_right, wo_left, stay, come, slices[1], slices[3], last = hold(
        payload, w_output, wo_right, wo_left, stay, come, slices[1], slices[3], pieces[2]
    )
    wo_all = [w_output, wo_right, shift_x(w_output, 2), wo_left]
    slices[2] = shift_y(last, 2)

    arrived = swap_z(payload)

    lower = jnp.where(c == 0, stay, come)
    upper = jnp.where(c == 0, come, stay)
    cache_out = jnp.concatenate([lower, upper], axis=1).reshape(32, 16, 4, 128)
    cache_out = jnp.transpose(cache_out, (0, 2, 1, 3)).reshape(32, 64, 128)
    arrived, cache_out = hold(arrived, cache_out)
    piece = finish(place[2:], arrived, own, new_bias)
    attended = swap_z(piece)
    attended_theirs = exchange_cores(attended)

    chunks = project(place, attended, attended_theirs, *wo_all)
    chunks, slices[2] = hold(chunks, slices[2])
    mid = early[:64].astype(F32) + lax.dynamic_index_in_dim(chunks, (x - y) % NX, 0, keepdims=False)
    chunks = chunks.astype(BF)
    for step in range(1, 4):
        sent = lax.dynamic_index_in_dim(chunks, (x - y - step) % NX, 0, keepdims=False)
        mid = mid + shift_y(sent, step).astype(F32)
    feature = (mid * early[64].astype(F32)[None, :]).astype(BF)
    square_parts = jnp.stack(parts_of(jnp.sum(mid * mid, axis=1)) + [jnp.zeros((64,), BF)] * 13)
    empty = jnp.zeros_like(square_parts)
    square_parts = jnp.where(
        x % 2 == 0,
        jnp.concatenate([square_parts, empty], axis=1),
        jnp.concatenate([empty, square_parts], axis=1),
    )
    payload = jnp.concatenate([feature, square_parts], axis=0)
    arrived = swap_zx(jnp.broadcast_to(payload[None], (32, 80, 128)))
    arrived_theirs = exchange_cores(arrived)

    both, squares, *sent = ffn_in(*slices, arrived, arrived_theirs)
    got = [shift_y(sent[step - 1], -step) for step in range(1, 4)]
    act = act_of(both, squares, *got)
    acts = [act] + [shift_y(act, step) for step in range(1, 4)]
    got = exchange_cores(down(1, *slices, *acts))
    arrived = swap_zx(down(0, *slices, *acts, got, cache_out))
    summed = jnp.sum(arrived[:, :64].astype(F32), axis=0)
    slot_cache = jnp.transpose(arrived[:, 64:].reshape(32, 4, 16, 128), (0, 2, 1, 3))

    sel_key = jnp.where(row_pos // DOC_LEN == mine, row_pos % DOC_LEN, -1)
    hits = sel_key[None, :] == jnp.arange(DOC_LEN, dtype=jnp.int32)[:, None]
    covered = jnp.any(hits, axis=1)
    new_own, new_others = own[:, 64:], others[:, 64:]
    new_flat = jnp.stack(
        [jnp.where(c == 0, new_own, new_others), jnp.where(c == 0, new_others, new_own)]
    ).reshape(2, 8, 2, 32, 128)
    new_flat = jnp.transpose(new_flat, (1, 3, 2, 0, 4)).reshape(ROWS, 512)
    placed = jnp.dot(hits.astype(BF), new_flat, preferred_element_type=F32).astype(BF)
    joined = jnp.where(covered[:, None], placed, slot_cache.reshape(DOC_LEN, 512))
    joined = joined.reshape(DOC_LEN, 2, 256)
    result = permute_xy((mid + summed).astype(BF), lambda a, b: (b, a))
    return (result, joined)


def solution(mesh):
    split = Mesh(mesh.devices.reshape(NZ, NX, NC, NY), ("z", "x", "c", "y"))
    pool = ("z", "x", "c")
    return jax.shard_map(
        shards,
        mesh=split,
        in_specs=(
            P(None, pool),
            P(None, pool, None, "y"),
            P(),
            P(),
            P(pool),
            P(pool, "y"),
            P(pool, None, "y"),
            P("y", pool),
            P(pool),
            P(None, None, ("z", "x", "c", "y")),
            P(("z", "x", "c", "y"), None),
        ),
        out_specs=(P("y", pool), P(pool, None, "y")),
        check_vma=False,
    )
```

```python
import functools

import jax
import jax.numpy as jnp
from jax import lax
from jax.experimental import pallas as pl
from jax.experimental.pallas import tpu as pltpu
from jax.sharding import Mesh
from jax.sharding import PartitionSpec as P

D = 8192
HEAD_DIM = 128
DOC_LEN = 512
SEL_DEV = 3
EPS = 1e-05
NEG = -1e30
FLOOR = -1e29
NZ, NX, NC, NY = 8, 4, 2, 4
POOL = NZ * NX * NC
ROWS = 256

BF = jnp.bfloat16
F32 = jnp.float32


def exchange_cores(value):
    return lax.ppermute(value, "c", [(0, 1), (1, 0)])


def shift_y(value, step):
    return lax.ppermute(value, "y", [(i, (i + step) % NY) for i in range(NY)])


def permute_xy(value, target):
    pairs = []
    for x in range(NX):
        for y in range(NY):
            to_x, to_y = target(x, y)
            pairs.append((x * NY + y, (to_x % NX) * NY + to_y % NY))
    return lax.ppermute(value, ("x", "y"), pairs)


def swap_zx(value):
    return lax.all_to_all(value, ("z", "x"), 0, 0, tiled=True)


def parts_of(value):
    high = lax.reduce_precision(value, 8, 7)
    rest = value - high
    middle = lax.reduce_precision(rest, 8, 7)
    low = rest - middle
    return [high.astype(BF), middle.astype(BF), low.astype(BF)]


def shift_x(value, step):
    return lax.ppermute(value, "x", [(i, (i + step) % NX) for i in range(NX)])


def swap_z(value):
    return lax.all_to_all(value, "z", 0, 0, tiled=True)


def hold(*values):
    return lax.optimization_barrier(values)


def positions(sel_index, doc_order):
    docs = jnp.arange(POOL, dtype=jnp.int32)
    slot_of_doc = jnp.sum(jnp.where(doc_order[:, None] == docs[None, :], docs[:, None], 0), axis=0)
    sel_doc = sel_index // DOC_LEN
    sel_tok = sel_index % DOC_LEN
    sel_slot = jnp.sum(
        jnp.where(sel_doc[:, None] == docs[None, :], slot_of_doc[None, :], 0), axis=1
    )
    sel_pos = sel_slot * DOC_LEN + sel_tok
    query_pos = DOC_LEN * POOL + docs
    row_pos = jnp.concatenate(
        [sel_pos.reshape(POOL, SEL_DEV), query_pos[:, None]], axis=1
    ).reshape(ROWS)
    return slot_of_doc, row_pos


def slices_kernel(place_ref, in_ref, out_ref, *pieces):
    core = place_ref[0]
    y = place_ref[1]
    for step in range(4):
        base = lax.rem(y + step, NY) * 256
        for rel in range(2):
            group = core if rel == 0 else 1 - core
            lanes = pl.ds(pl.multiple_of(base + group * 128, 128), 128)
            pieces[step][0, rel, 0:224, :] = in_ref[:, lanes]
            pieces[step][0, rel, 224:336, :] = out_ref[:, lanes]


def weight_slices(place, flat_in, w_out):
    return pl.pallas_call(
        slices_kernel,
        grid=(NZ,),
        out_shape=tuple(jax.ShapeDtypeStruct((NZ, 2, 336, 128), BF) for _ in range(4)),
        in_specs=[
            pl.BlockSpec(memory_space=pltpu.SMEM),
            pl.BlockSpec((224, 1024), lambda k: (0, k)),
            pl.BlockSpec((112, 1024), lambda k: (0, k)),
        ],
        out_specs=tuple(pl.BlockSpec((1, 2, 336, 128), lambda k: (k, 0, 0, 0)) for _ in range(4)),
        compiler_params=pltpu.CompilerParams(vmem_limit_bytes=8 * 1024 * 1024),
        cost_estimate=pl.CostEstimate(flops=0, bytes_accessed=11_000_000, transcendentals=0),
        name="weight_slices",
    )(place, flat_in, w_out)


NT = (((1,), (1,)), ((), ()))
TN = (((0,), (0,)), ((), ()))


def split_rows(value):
    high = value.astype(BF).astype(F32)
    rest = value - high
    middle = rest.astype(BF).astype(F32)
    return [high, middle, rest - middle]


VMEM = pl.BlockSpec(memory_space=pltpu.VMEM)
SMEM = pl.BlockSpec(memory_space=pltpu.SMEM)


def grant(mib):
    return pltpu.CompilerParams(vmem_limit_bytes=mib * 1024 * 1024)


def scale_kernel(in_ref, out_ref):
    value = in_ref[0].astype(F32)
    for k in range(1, 32):
        value = value + in_ref[k].astype(F32)
    squares = value[128:129] + (value[129:130] + value[130:131])
    factor = jnp.broadcast_to(lax.rsqrt(squares / D + EPS), (8, 128)).T
    by_x = factor[0:64, 0:1]
    by_z = factor[64:96, 0:1]
    result = jnp.concatenate(
        [value[0:64] * by_x, value[64:96] * by_z, value[96:128] * by_z], axis=0
    ).astype(BF)
    for k in range(NZ):
        out_ref[k] = result


def scale(value):
    return pl.pallas_call(
        scale_kernel,
        out_shape=jax.ShapeDtypeStruct((NZ, 128, 128), BF),
        in_specs=[VMEM],
        out_specs=VMEM,
        compiler_params=grant(6),
        cost_estimate=pl.CostEstimate(flops=600_000, bytes_accessed=1_500_000, transcendentals=0),
        name="scale",
    )(value)


def attend_kernel(
    place_ref, bias_ref, own_ref, other_ref, c0, c1, c2, c3, acc_ref, sent_ref, stat_ref
):
    core = place_ref[0]
    blocks = (c0, c1, c2, c3)
    for rel in range(2):
        query_ref = own_ref if rel == 0 else other_ref
        group = core if rel == 0 else 1 - core
        key_at = pl.ds(pl.multiple_of(group * 128, 128), 128)
        value_at = pl.ds(pl.multiple_of(256 + group * 128, 128), 128)
        for half in range(2):
            lanes = slice(half * 256, half * 256 + 256)
            query = jnp.concatenate(
                [query_ref[half * 4 + i, 0:64, :] for i in range(4)], axis=0
            )
            scores = []
            top = jnp.full((1, 256), FLOOR, F32)
            for k in range(4):
                bias = bias_ref[k * 512 : k * 512 + 512, :].astype(F32)
                part = lax.dot_general(
                    blocks[k][:, key_at], query, NT, preferred_element_type=F32
                ) * (HEAD_DIM**-0.5) + jnp.concatenate([bias, bias], axis=1)
                scores.append(part)
                top = jnp.maximum(top, jnp.max(part, axis=0, keepdims=True))
            total = jnp.zeros((1, 256), F32)
            acc = jnp.zeros((128, 256), F32)
            for k in range(4):
                probs = jnp.exp(scores[k] - top)
                total = total + jnp.sum(probs, axis=0, keepdims=True)
                acc = acc + lax.dot_general(
                    blocks[k][:, value_at], probs.astype(BF), TN, preferred_element_type=F32
                )
            if rel == 0:
                acc_ref[:, lanes] = acc
                stat_ref[0:1, lanes] = top
                stat_ref[1:2, lanes] = total
            else:
                stats = split_rows(top) + split_rows(total) + [jnp.zeros((10, 256), F32)]
                sent_ref[0:128, lanes] = acc.astype(BF)
                sent_ref[128:144, lanes] = jnp.concatenate(stats, axis=0).astype(BF)


def attend(place, bias, own, other, blocks):
    vmem = pl.BlockSpec(memory_space=pltpu.VMEM)
    return pl.pallas_call(
        attend_kernel,
        out_shape=(
            jax.ShapeDtypeStruct((128, 512), F32),
            jax.ShapeDtypeStruct((144, 512), BF),
            jax.ShapeDtypeStruct((8, 512), F32),
        ),
        in_specs=[pl.BlockSpec(memory_space=pltpu.SMEM)] + [vmem] * 7,
        out_specs=(vmem, vmem, vmem),
        compiler_params=pltpu.CompilerParams(vmem_limit_bytes=16 * 1024 * 1024),
        cost_estimate=pl.CostEstimate(
            flops=2 * 16 * 2 * 2048 * 128 * 64, bytes_accessed=6_000_000, transcendentals=2097152
        ),
        name="attend",
    )(place, bias, own, other, *blocks)


def merge_kernel(acc_ref, stat_ref, far_ref, out_ref):
    near_top = stat_ref[0:1, :]
    stat = far_ref[128:144, :].astype(F32)
    far_top = stat[0:1] + (stat[1:2] + stat[2:3])
    far_total = stat[3:4] + (stat[4:5] + stat[5:6])
    top = jnp.maximum(near_top, far_top)
    near = jnp.exp(near_top - top)
    far = jnp.exp(far_top - top)
    total = stat_ref[1:2, :] * near + far_total * far
    acc = acc_ref[...] * near + far_ref[0:128, :].astype(F32) * far
    rows = acc.T.astype(BF)
    stats = split_rows(top) + split_rows(total) + [jnp.zeros((10, 512), F32)]
    stats = jnp.concatenate(stats, axis=0).astype(BF)
    for head in range(8):
        pair = head // 2
        out_ref[head, 0:64, :] = rows[head * 64 : head * 64 + 64, :]
        out_ref[head, 64:80, :] = stats[:, pair * 128 : pair * 128 + 128]


def merge(*operands):
    return pl.pallas_call(
        merge_kernel,
        out_shape=jax.ShapeDtypeStruct((8, 80, 128), BF),
        in_specs=[VMEM] * 3,
        out_specs=VMEM,
        cost_estimate=pl.CostEstimate(flops=500_000, bytes_accessed=1_000_000, transcendentals=0),
        compiler_params=pltpu.CompilerParams(vmem_limit_bytes=6 * 1024 * 1024),
        name="merge",
    )(*operands)


def finish_kernel(
    place_ref, arrived_ref, own_ref, bias_ref, out_ref, column_ref, new_ref
):
    z = place_ref[2]
    keys = jnp.concatenate([own_ref[k, 64:96, :] for k in range(8)], axis=0)
    values = jnp.concatenate([own_ref[k, 96:128, :] for k in range(8)], axis=0)
    query = own_ref[z, 0:64, :]
    query = jnp.concatenate([query, query], axis=0)
    scores = lax.dot_general(keys, query, NT, preferred_element_type=F32)
    scores = scores * (HEAD_DIM**-0.5) + bias_ref[...].astype(F32)
    tops = []
    sums = []
    for k in range(8):
        stat = arrived_ref[k, 64:80, :].astype(F32)
        tops.append(stat[0:1] + (stat[1:2] + stat[2:3]))
        sums.append(stat[3:4] + (stat[4:5] + stat[5:6]))
    tops = jnp.concatenate(tops, axis=0)
    sums = jnp.concatenate(sums, axis=0)
    top = jnp.maximum(
        jnp.max(tops, axis=0, keepdims=True), jnp.max(scores, axis=0, keepdims=True)
    )
    by = jnp.exp(tops - top)
    probs = jnp.exp(scores - top)
    norm = jnp.sum(sums * by, axis=0, keepdims=True) + jnp.sum(probs, axis=0, keepdims=True)
    column_ref[...] = jnp.concatenate([by, jnp.broadcast_to(norm, (8, 128))], axis=0).T
    new_ref[...] = lax.dot_general(
        probs.astype(BF), values, TN, preferred_element_type=F32
    )
    mine = pl.ds(pl.multiple_of(lax.rem(z, 2) * 64, 64), 64)
    column = column_ref[mine, :]
    acc = new_ref[mine, :]
    for k in range(8):
        acc = acc + arrived_ref[k, 0:64, :].astype(F32) * column[:, k : k + 1]
    result = (acc / column[:, 8:9]).astype(BF)
    for k in range(8):
        out_ref[k] = result


def finish(*operands):
    return pl.pallas_call(
        finish_kernel,
        out_shape=jax.ShapeDtypeStruct((8, 64, 128), BF),
        in_specs=[SMEM] + [VMEM] * 3,
        out_specs=VMEM,
        scratch_shapes=[pltpu.VMEM((128, 16), F32), pltpu.VMEM((128, 128), F32)],
        cost_estimate=pl.CostEstimate(flops=20_000_000, bytes_accessed=800_000, transcendentals=0),
        compiler_params=pltpu.CompilerParams(vmem_limit_bytes=6 * 1024 * 1024),
        name="finish",
    )(*operands)


def project_kernel(place_ref, own_ref, far_ref, w0, w1, w2, w3, keep_ref, out_ref):
    core = place_ref[0]
    y = place_ref[1]
    x = place_ref[3]
    for k, weight_ref in enumerate((w0, w1, w2, w3)):
        value = jnp.zeros((64, 128), F32)
        for rel, ref in enumerate((own_ref, far_ref)):
            group = core if rel == 0 else 1 - core
            at = pl.ds(pl.multiple_of(group * 1024, 1024), 1024)
            rows = jnp.concatenate([ref[i] for i in range(8)], axis=1)
            value = value + jnp.dot(rows, weight_ref[at, :], preferred_element_type=F32)
        step = lax.rem(x - y - k + 2 * NX, NX)
        out_ref[step] = value.astype(BF)

        @pl.when(step == 0)
        def _():
            keep_ref[...] = value


def project(*operands):
    return pl.pallas_call(
        project_kernel,
        out_shape=(
            jax.ShapeDtypeStruct((64, 128), F32),
            jax.ShapeDtypeStruct((NX, 64, 128), BF),
        ),
        in_specs=[SMEM] + [VMEM] * 6,
        out_specs=(VMEM, VMEM),
        compiler_params=grant(8),
        cost_estimate=pl.CostEstimate(
            flops=2 * 64 * 2048 * 512, bytes_accessed=2_500_000, transcendentals=0
        ),
        name="project",
    )(*operands)


def middle_kernel(place_ref, keep_ref, r1, r2, r3, early_ref, mid_ref, out_ref):
    x = place_ref[3]
    mid = early_ref[0:64, :].astype(F32) + keep_ref[...]
    for ref in (r1, r2, r3):
        mid = mid + ref[...].astype(F32)
    mid_ref[...] = mid
    gain = early_ref[64:80, :].astype(F32)[0:1]
    feature = (mid * gain).astype(BF)
    both = jnp.concatenate([mid, mid], axis=0)
    squares = jnp.sum((both * both).T, axis=0, keepdims=True)
    lane = lax.broadcasted_iota(jnp.int32, (1, 128), 1)
    squares = jnp.where(lane // 64 == lax.rem(x, 2), squares, 0.0)
    rows = jnp.concatenate(split_rows(squares) + [jnp.zeros((13, 128), F32)], axis=0).astype(BF)
    for k in range(32):
        out_ref[k, 0:64, :] = feature
        out_ref[k, 64:80, :] = rows


def middle(*operands):
    return pl.pallas_call(
        middle_kernel,
        out_shape=(
            jax.ShapeDtypeStruct((64, 128), F32),
            jax.ShapeDtypeStruct((32, 80, 128), BF),
        ),
        in_specs=[SMEM] + [VMEM] * 5,
        out_specs=(VMEM, VMEM),
        compiler_params=grant(6),
        cost_estimate=pl.CostEstimate(flops=100_000, bytes_accessed=800_000, transcendentals=0),
        name="middle",
    )(*operands)


def ffn_in_kernel(p0, p1, p2, p3, own_ref, far_ref, keep_ref, square_ref, s1, s2, s3, feature):
    pairs = [jnp.zeros((1, 128), F32), jnp.zeros((1, 128), F32)]
    for rel, ref in enumerate((own_ref, far_ref)):
        for z in range(NZ):
            for k in range(4):
                feature[rel, k * 64 : k * 64 + 64, z * 128 : z * 128 + 128] = ref[
                    z * 4 + k, 0:64, :
                ]
                stat = ref[z * 4 + k, 64:80, :].astype(F32)
                pairs[k // 2] = pairs[k // 2] + (stat[0:1] + (stat[1:2] + stat[2:3]))
    squares = jnp.concatenate(pairs, axis=1)
    square_ref[...] = jnp.broadcast_to(squares, (8, ROWS))
    rows = jnp.concatenate(split_rows(squares) + [jnp.zeros((13, ROWS), F32)], axis=0).astype(BF)
    for step, (piece, to) in enumerate(((p1, s1), (p2, s2), (p3, s3), (p0, keep_ref))):
        value = jnp.zeros((224, ROWS), F32)
        for rel in range(2):
            weight = jnp.concatenate([piece[z, rel, 0:224, :] for z in range(NZ)], axis=1)
            value = value + lax.dot_general(weight, feature[rel], NT, preferred_element_type=F32)
        if step < 3:
            to[0:224, :] = value.astype(BF)
            to[224:240, :] = rows
        else:
            to[...] = value


def ffn_in(*operands):
    sent = jax.ShapeDtypeStruct((240, ROWS), BF)
    return pl.pallas_call(
        ffn_in_kernel,
        out_shape=(
            jax.ShapeDtypeStruct((224, ROWS), F32),
            jax.ShapeDtypeStruct((8, ROWS), F32),
            sent,
            sent,
            sent,
        ),
        in_specs=[VMEM] * 6,
        out_specs=(VMEM,) * 5,
        scratch_shapes=[pltpu.VMEM((2, ROWS, 1024), BF)],
        compiler_params=pltpu.CompilerParams(vmem_limit_bytes=16 * 1024 * 1024),
        cost_estimate=pl.CostEstimate(
            flops=2 * 896 * 2048 * 256, bytes_accessed=7_500_000, transcendentals=0
        ),
        name="ffn_in",
    )(*operands)


def act_kernel(both_ref, square_ref, r1, r2, r3, out_ref):
    both = both_ref[...]
    squares = square_ref[0:1, :]
    for ref in (r1, r2, r3):
        both = both + ref[0:224, :].astype(F32)
        stat = ref[224:240, :].astype(F32)
        squares = squares + (stat[0:1] + (stat[1:2] + stat[2:3]))
    both = both * lax.rsqrt(squares / D + EPS)
    gate = both[0:112]
    out_ref[...] = (gate / (1.0 + jnp.exp(-gate)) * both[112:224]).astype(BF)


def act_of(*operands):
    return pl.pallas_call(
        act_kernel,
        out_shape=jax.ShapeDtypeStruct((112, ROWS), BF),
        in_specs=[VMEM] * 5,
        out_specs=VMEM,
        cost_estimate=pl.CostEstimate(flops=500_000, bytes_accessed=700_000, transcendentals=0),
        compiler_params=pltpu.CompilerParams(vmem_limit_bytes=6 * 1024 * 1024),
        name="act",
    )(*operands)


def down_kernel(rel, p0, p1, p2, p3, a0, a1, a2, a3, *refs):
    act = jnp.concatenate([a0[...], a1[...], a2[...], a3[...]], axis=0)
    weight = jnp.concatenate(
        [
            jnp.concatenate([p[z, rel, 224:336, :] for z in range(NZ)], axis=1)
            for p in (p0, p1, p2, p3)
        ],
        axis=0,
    )
    term = lax.dot_general(act, weight, TN, preferred_element_type=F32)
    for z in range(NZ):
        block = term[:, z * 128 : z * 128 + 128]
        if rel == 1:
            refs[-1][z] = block.astype(BF)
        else:
            block = (block + refs[0][z].astype(F32)).astype(BF)
            for k in range(NX):
                refs[-1][z * NX + k, 0:64, :] = block[k * 64 : k * 64 + 64, :]
                refs[-1][z * NX + k, 64:128, :] = refs[1][z * NX + k]


def down(rel, *operands):
    return pl.pallas_call(
        functools.partial(down_kernel, rel),
        out_shape=jax.ShapeDtypeStruct((NZ, ROWS, 128) if rel else (32, 128, 128), BF),
        in_specs=[VMEM] * len(operands),
        out_specs=VMEM,
        compiler_params=pltpu.CompilerParams(vmem_limit_bytes=16 * 1024 * 1024),
        cost_estimate=pl.CostEstimate(
            flops=448 * 2048 * 256, bytes_accessed=4_000_000, transcendentals=0
        ),
        name="down",
    )(*operands)


def shards(
    hidden_rows,
    cache_kv,
    sel_index,
    doc_order,
    attn_gain,
    w_query,
    w_keyval,
    w_output,
    ffn_gain,
    w_in,
    w_out,
):
    z, x, c, y = (lax.axis_index(name) for name in ("z", "x", "c", "y"))
    mine = (z * NX + x) * NC + c
    other = 1 - c

    def half(group):
        return jnp.concatenate(
            [
                lax.dynamic_slice_in_dim(w_query, group * 1024, 1024, 1),
                lax.dynamic_slice_in_dim(w_keyval[:, 0], group * 128, 128, 1),
                lax.dynamic_slice_in_dim(w_keyval[:, 1], group * 128, 128, 1),
            ],
            axis=1,
        )

    place = jnp.stack([c, y, z, x]).astype(jnp.int32)

    early = jnp.concatenate(
        [
            lax.dynamic_slice_in_dim(hidden_rows, y * 64, 64, 0),
            jnp.broadcast_to(ffn_gain[None, :], (16, 128)),
        ],
        axis=0,
    )
    early = permute_xy(early, lambda a, b: (b, a))

    message = jnp.concatenate(
        [hidden_rows, jnp.broadcast_to(attn_gain[None, :], (16, 128))], axis=0
    )
    theirs = exchange_cores(message)
    weight_theirs = exchange_cores(half(other))

    theirs, raw = hold(theirs, cache_kv)
    cache = raw.reshape(DOC_LEN, 512)

    weight = jnp.concatenate([half(c), weight_theirs], axis=0)
    inputs = jnp.concatenate([hidden_rows, theirs[:ROWS]], axis=1).astype(F32)
    gain = jnp.concatenate([attn_gain, theirs[ROWS]], axis=0).astype(F32)
    squares = jnp.sum(inputs * inputs, axis=1)
    scaled = (inputs * gain[None, :]).astype(BF)
    partial = jnp.dot(scaled, weight, preferred_element_type=F32).astype(BF)
    query_part = jnp.transpose(partial[:, :1024].reshape(4, 64, 8, 128), (2, 0, 1, 3))
    new_part = jnp.transpose(partial[:, 1024:].reshape(8, 32, 2, 128), (0, 2, 1, 3))
    square_parts = jnp.stack(parts_of(squares) + [jnp.zeros((ROWS,), BF)] * 5)
    by_x = jnp.transpose(square_parts.reshape(8, 4, 64), (1, 0, 2))
    by_z = jnp.transpose(square_parts.reshape(8, 8, 32), (1, 0, 2))
    square_parts = jnp.concatenate(
        [
            jnp.broadcast_to(by_x[None], (8, 4, 8, 64)),
            jnp.broadcast_to(by_z[:, None], (8, 4, 8, 32)),
            jnp.zeros((8, 4, 8, 32), BF),
        ],
        axis=3,
    )
    new_part = jnp.broadcast_to(new_part.reshape(8, 1, 64, 128), (8, 4, 64, 128))
    payload = jnp.concatenate([query_part, new_part, square_parts], axis=2).reshape(32, 136, 128)

    payload, cache, sel_index, doc_order, early = hold(
        payload, cache, sel_index, doc_order, early
    )
    reordered = cache.reshape(POOL, 8, 512).at[doc_order].get(mode="promise_in_bounds")
    reordered = reordered.reshape(32, 2, 8, 512)
    stay = lax.dynamic_index_in_dim(reordered, c, 1, keepdims=False)
    leave = lax.dynamic_index_in_dim(reordered, other, 1, keepdims=False)
    come, w_in, w_out = hold(exchange_cores(leave), w_in, w_out)
    right, left, across = shift_x(cache, 1), shift_x(cache, -1), shift_x(cache, 2)
    arrived, right, left, across = hold(swap_zx(payload), right, left, across)
    piece = scale(arrived)

    flat_in = jnp.transpose(w_in, (1, 2, 0)).reshape(224, D)
    pieces = weight_slices(place, flat_in, w_out)
    slices = [pieces[0], shift_y(pieces[1], 1), None, shift_y(pieces[3], 3)]

    slot_of_doc, row_pos = positions(sel_index, doc_order)
    my_pos = lax.dynamic_slice_in_dim(row_pos, x * 64, 64, 0)
    my_pos = jnp.concatenate([my_pos, my_pos])[None, :]
    token = jnp.arange(8, dtype=jnp.int32)
    docs = jnp.arange(POOL, dtype=jnp.int32)
    key_pos = []
    for step in (0, 1, 3, 2):
        base = ((z * NX + (x - step) % NX) * NC + c) * 8
        name = (docs[:, None] * DOC_LEN + base + token[None, :]).reshape(DOC_LEN)
        at = (slot_of_doc[:, None] * DOC_LEN + base + token[None, :]).reshape(DOC_LEN)
        written = jnp.any(name[:, None] == sel_index[None, :], axis=1)
        key_pos.append(jnp.where(written, DOC_LEN * POOL * 2, at))
    bias = jnp.where(jnp.concatenate(key_pos)[:, None] <= my_pos, 0.0, NEG).astype(BF)
    new_bias = jnp.where(row_pos[:, None] <= my_pos, 0.0, NEG).astype(BF)

    piece, bias, new_bias, pieces, w_output = hold(piece, bias, new_bias, pieces, w_output)
    own = swap_z(piece)
    wo_right, wo_left = shift_x(w_output, 1), shift_x(w_output, -1)
    others = exchange_cores(own)
    acc, acc_sent, stats = attend(place, bias, own, others, (cache, right, left, across))

    payload = merge(acc, stats, exchange_cores(acc_sent))
    payload, w_output, wo_right, wo_left, stay, come, slices[1], slices[3], last = hold(
        payload, w_output, wo_right, wo_left, stay, come, slices[1], slices[3], pieces[2]
    )
    wo_all = [w_output, wo_right, shift_x(w_output, 2), wo_left]
    slices[2] = shift_y(last, 2)

    arrived = swap_z(payload)

    piece = finish(place, arrived, own, new_bias)
    attended = swap_z(piece)
    attended_theirs = exchange_cores(attended)

    keep, chunks = project(place, attended, attended_theirs, *wo_all)
    keep, chunks, slices[2] = hold(keep, chunks, slices[2])
    got = [shift_y(chunks[step], step) for step in range(1, 4)]
    mid, payload = middle(place, keep, *got, early)
    payload, stay, come = hold(payload, stay, come)

    lower = jnp.where(c == 0, stay, come)
    upper = jnp.where(c == 0, come, stay)
    cache_out = jnp.concatenate([lower, upper], axis=1).reshape(32, 16, 4, 128)
    cache_out = jnp.transpose(cache_out, (0, 2, 1, 3)).reshape(32, 64, 128)
    arrived, cache_out = hold(swap_zx(payload), cache_out)
    arrived_theirs = exchange_cores(arrived)

    both, squares, *sent = ffn_in(*slices, arrived, arrived_theirs)
    got = [shift_y(sent[step - 1], -step) for step in range(1, 4)]
    act = act_of(both, squares, *got)
    acts = [act] + [shift_y(act, step) for step in range(1, 4)]
    got = exchange_cores(down(1, *slices, *acts))
    arrived = swap_zx(down(0, *slices, *acts, got, cache_out))
    summed = jnp.sum(arrived[:, :64].astype(F32), axis=0)
    slot_cache = jnp.transpose(arrived[:, 64:].reshape(32, 4, 16, 128), (0, 2, 1, 3))

    sel_key = jnp.where(row_pos // DOC_LEN == mine, row_pos % DOC_LEN, -1)
    hits = sel_key[None, :] == jnp.arange(DOC_LEN, dtype=jnp.int32)[:, None]
    covered = jnp.any(hits, axis=1)
    new_own, new_others = own[:, 64:], others[:, 64:]
    new_flat = jnp.stack(
        [jnp.where(c == 0, new_own, new_others), jnp.where(c == 0, new_others, new_own)]
    ).reshape(2, 8, 2, 32, 128)
    new_flat = jnp.transpose(new_flat, (1, 3, 2, 0, 4)).reshape(ROWS, 512)
    placed = jnp.dot(hits.astype(BF), new_flat, preferred_element_type=F32).astype(BF)
    joined = jnp.where(covered[:, None], placed, slot_cache.reshape(DOC_LEN, 512))
    joined = joined.reshape(DOC_LEN, 2, 256)
    result = permute_xy((mid + summed).astype(BF), lambda a, b: (b, a))
    return (result, joined)


def solution(mesh):
    split = Mesh(mesh.devices.reshape(NZ, NX, NC, NY), ("z", "x", "c", "y"))
    pool = ("z", "x", "c")
    return jax.shard_map(
        shards,
        mesh=split,
        in_specs=(
            P(None, pool),
            P(None, pool, None, "y"),
            P(),
            P(),
            P(pool),
            P(pool, "y"),
            P(pool, None, "y"),
            P("y", pool),
            P(pool),
            P(None, None, ("z", "x", "c", "y")),
            P(("z", "x", "c", "y"), None),
        ),
        out_specs=(P("y", pool), P(pool, None, "y")),
        check_vma=False,
    )
```

```python
import functools

import jax
import jax.numpy as jnp
from jax import lax
from jax.experimental import pallas as pl
from jax.experimental.pallas import tpu as pltpu
from jax.sharding import Mesh
from jax.sharding import PartitionSpec as P

D = 8192
HEAD_DIM = 128
DOC_LEN = 512
SEL_DEV = 3
EPS = 1e-05
NEG = -1e30
FLOOR = -1e29
NZ, NX, NC, NY = 8, 4, 2, 4
POOL = NZ * NX * NC
ROWS = 256

BF = jnp.bfloat16
F32 = jnp.float32


def exchange_cores(value):
    return lax.ppermute(value, "c", [(0, 1), (1, 0)])


def shift_y(value, step):
    return lax.ppermute(value, "y", [(i, (i + step) % NY) for i in range(NY)])


def permute_xy(value, target):
    pairs = []
    for x in range(NX):
        for y in range(NY):
            to_x, to_y = target(x, y)
            pairs.append((x * NY + y, (to_x % NX) * NY + to_y % NY))
    return lax.ppermute(value, ("x", "y"), pairs)


def swap_zx(value):
    return lax.all_to_all(value, ("z", "x"), 0, 0, tiled=True)


def parts_of(value):
    high = lax.reduce_precision(value, 8, 7)
    rest = value - high
    middle = lax.reduce_precision(rest, 8, 7)
    low = rest - middle
    return [high.astype(BF), middle.astype(BF), low.astype(BF)]


def shift_x(value, step):
    return lax.ppermute(value, "x", [(i, (i + step) % NX) for i in range(NX)])


def swap_z(value):
    return lax.all_to_all(value, "z", 0, 0, tiled=True)


def hold(*values):
    return lax.optimization_barrier(values)


def positions(sel_index, doc_order):
    docs = jnp.arange(POOL, dtype=jnp.int32)
    slot_of_doc = jnp.sum(jnp.where(doc_order[:, None] == docs[None, :], docs[:, None], 0), axis=0)
    sel_doc = sel_index // DOC_LEN
    sel_tok = sel_index % DOC_LEN
    sel_slot = jnp.sum(
        jnp.where(sel_doc[:, None] == docs[None, :], slot_of_doc[None, :], 0), axis=1
    )
    sel_pos = sel_slot * DOC_LEN + sel_tok
    query_pos = DOC_LEN * POOL + docs
    row_pos = jnp.concatenate(
        [sel_pos.reshape(POOL, SEL_DEV), query_pos[:, None]], axis=1
    ).reshape(ROWS)
    return slot_of_doc, row_pos


def slices_kernel(place_ref, in_ref, out_ref, *pieces):
    core = place_ref[0]
    y = place_ref[1]
    for step in range(4):
        base = lax.rem(y + step, NY) * 256
        for rel in range(2):
            group = core if rel == 0 else 1 - core
            lanes = pl.ds(pl.multiple_of(base + group * 128, 128), 128)
            pieces[step][0, rel, 0:224, :] = in_ref[:, lanes]
            pieces[step][0, rel, 224:336, :] = out_ref[:, lanes]


def weight_slices(place, flat_in, w_out):
    return pl.pallas_call(
        slices_kernel,
        grid=(NZ,),
        out_shape=tuple(jax.ShapeDtypeStruct((NZ, 2, 336, 128), BF) for _ in range(4)),
        in_specs=[
            pl.BlockSpec(memory_space=pltpu.SMEM),
            pl.BlockSpec((224, 1024), lambda k: (0, k)),
            pl.BlockSpec((112, 1024), lambda k: (0, k)),
        ],
        out_specs=tuple(pl.BlockSpec((1, 2, 336, 128), lambda k: (k, 0, 0, 0)) for _ in range(4)),
        compiler_params=pltpu.CompilerParams(vmem_limit_bytes=8 * 1024 * 1024),
        cost_estimate=pl.CostEstimate(flops=0, bytes_accessed=11_000_000, transcendentals=0),
        name="weight_slices",
    )(place, flat_in, w_out)


NT = (((1,), (1,)), ((), ()))
TN = (((0,), (0,)), ((), ()))


def split_rows(value):
    high = value.astype(BF).astype(F32)
    rest = value - high
    middle = rest.astype(BF).astype(F32)
    return [high, middle, rest - middle]


VMEM = pl.BlockSpec(memory_space=pltpu.VMEM)
SMEM = pl.BlockSpec(memory_space=pltpu.SMEM)


def grant(mib):
    return pltpu.CompilerParams(vmem_limit_bytes=mib * 1024 * 1024)


def scale_kernel(in_ref, out_ref):
    value = in_ref[0].astype(F32)
    for k in range(1, 32):
        value = value + in_ref[k].astype(F32)
    squares = value[128:129] + (value[129:130] + value[130:131])
    factor = jnp.broadcast_to(lax.rsqrt(squares / D + EPS), (8, 128)).T
    by_x = factor[0:64, 0:1]
    by_z = factor[64:96, 0:1]
    result = jnp.concatenate(
        [value[0:64] * by_x, value[64:96] * by_z, value[96:128] * by_z], axis=0
    ).astype(BF)
    for k in range(NZ):
        out_ref[k] = result


def scale(value):
    return pl.pallas_call(
        scale_kernel,
        out_shape=jax.ShapeDtypeStruct((NZ, 128, 128), BF),
        in_specs=[VMEM],
        out_specs=VMEM,
        compiler_params=grant(6),
        cost_estimate=pl.CostEstimate(flops=600_000, bytes_accessed=1_500_000, transcendentals=0),
        name="scale",
    )(value)


def attend_kernel(
    place_ref, bias_ref, own_ref, other_ref, c0, c1, c2, c3, acc_ref, sent_ref, stat_ref
):
    core = place_ref[0]
    blocks = (c0, c1, c2, c3)
    for rel in range(2):
        query_ref = own_ref if rel == 0 else other_ref
        group = core if rel == 0 else 1 - core
        key_at = pl.ds(pl.multiple_of(group * 128, 128), 128)
        value_at = pl.ds(pl.multiple_of(256 + group * 128, 128), 128)
        for half in range(2):
            lanes = slice(half * 256, half * 256 + 256)
            query = jnp.concatenate(
                [query_ref[half * 4 + i, 0:64, :] for i in range(4)], axis=0
            )
            scores = []
            top = jnp.full((1, 256), FLOOR, F32)
            for k in range(4):
                bias = bias_ref[k * 512 : k * 512 + 512, :].astype(F32)
                part = lax.dot_general(
                    blocks[k][:, key_at], query, NT, preferred_element_type=F32
                ) * (HEAD_DIM**-0.5) + jnp.concatenate([bias, bias], axis=1)
                scores.append(part)
                top = jnp.maximum(top, jnp.max(part, axis=0, keepdims=True))
            total = jnp.zeros((1, 256), F32)
            acc = jnp.zeros((128, 256), F32)
            for k in range(4):
                probs = jnp.exp(scores[k] - top)
                total = total + jnp.sum(probs, axis=0, keepdims=True)
                acc = acc + lax.dot_general(
                    blocks[k][:, value_at], probs.astype(BF), TN, preferred_element_type=F32
                )
            if rel == 0:
                acc_ref[:, lanes] = acc
                stat_ref[0:1, lanes] = top
                stat_ref[1:2, lanes] = total
            else:
                stats = split_rows(top) + split_rows(total) + [jnp.zeros((10, 256), F32)]
                sent_ref[0:128, lanes] = acc.astype(BF)
                sent_ref[128:144, lanes] = jnp.concatenate(stats, axis=0).astype(BF)


def attend(place, bias, own, other, blocks):
    vmem = pl.BlockSpec(memory_space=pltpu.VMEM)
    return pl.pallas_call(
        attend_kernel,
        out_shape=(
            jax.ShapeDtypeStruct((128, 512), F32),
            jax.ShapeDtypeStruct((144, 512), BF),
            jax.ShapeDtypeStruct((8, 512), F32),
        ),
        in_specs=[pl.BlockSpec(memory_space=pltpu.SMEM)] + [vmem] * 7,
        out_specs=(vmem, vmem, vmem),
        compiler_params=pltpu.CompilerParams(vmem_limit_bytes=16 * 1024 * 1024),
        cost_estimate=pl.CostEstimate(
            flops=2 * 16 * 2 * 2048 * 128 * 64, bytes_accessed=6_000_000, transcendentals=2097152
        ),
        name="attend",
    )(place, bias, own, other, *blocks)


def merge_kernel(acc_ref, stat_ref, far_ref, out_ref):
    near_top = stat_ref[0:1, :]
    stat = far_ref[128:144, :].astype(F32)
    far_top = stat[0:1] + (stat[1:2] + stat[2:3])
    far_total = stat[3:4] + (stat[4:5] + stat[5:6])
    top = jnp.maximum(near_top, far_top)
    near = jnp.exp(near_top - top)
    far = jnp.exp(far_top - top)
    total = stat_ref[1:2, :] * near + far_total * far
    acc = acc_ref[...] * near + far_ref[0:128, :].astype(F32) * far
    rows = acc.T.astype(BF)
    stats = split_rows(top) + split_rows(total) + [jnp.zeros((10, 512), F32)]
    stats = jnp.concatenate(stats, axis=0).astype(BF)
    for head in range(8):
        pair = head // 2
        out_ref[head, 0:64, :] = rows[head * 64 : head * 64 + 64, :]
        out_ref[head, 64:80, :] = stats[:, pair * 128 : pair * 128 + 128]


def merge(*operands):
    return pl.pallas_call(
        merge_kernel,
        out_shape=jax.ShapeDtypeStruct((8, 80, 128), BF),
        in_specs=[VMEM] * 3,
        out_specs=VMEM,
        cost_estimate=pl.CostEstimate(flops=500_000, bytes_accessed=1_000_000, transcendentals=0),
        compiler_params=pltpu.CompilerParams(vmem_limit_bytes=6 * 1024 * 1024),
        name="merge",
    )(*operands)


def finish_kernel(
    place_ref, arrived_ref, own_ref, bias_ref, out_ref, column_ref, new_ref
):
    z = place_ref[2]
    keys = jnp.concatenate([own_ref[k, 64:96, :] for k in range(8)], axis=0)
    values = jnp.concatenate([own_ref[k, 96:128, :] for k in range(8)], axis=0)
    query = own_ref[z, 0:64, :]
    query = jnp.concatenate([query, query], axis=0)
    scores = lax.dot_general(keys, query, NT, preferred_element_type=F32)
    scores = scores * (HEAD_DIM**-0.5) + bias_ref[...].astype(F32)
    tops = []
    sums = []
    for k in range(8):
        stat = arrived_ref[k, 64:80, :].astype(F32)
        tops.append(stat[0:1] + (stat[1:2] + stat[2:3]))
        sums.append(stat[3:4] + (stat[4:5] + stat[5:6]))
    tops = jnp.concatenate(tops, axis=0)
    sums = jnp.concatenate(sums, axis=0)
    top = jnp.maximum(
        jnp.max(tops, axis=0, keepdims=True), jnp.max(scores, axis=0, keepdims=True)
    )
    by = jnp.exp(tops - top)
    probs = jnp.exp(scores - top)
    norm = jnp.sum(sums * by, axis=0, keepdims=True) + jnp.sum(probs, axis=0, keepdims=True)
    column_ref[...] = jnp.concatenate([by, jnp.broadcast_to(norm, (8, 128))], axis=0).T
    new_ref[...] = lax.dot_general(
        probs.astype(BF), values, TN, preferred_element_type=F32
    )
    mine = pl.ds(pl.multiple_of(lax.rem(z, 2) * 64, 64), 64)
    column = column_ref[mine, :]
    acc = new_ref[mine, :]
    for k in range(8):
        acc = acc + arrived_ref[k, 0:64, :].astype(F32) * column[:, k : k + 1]
    result = (acc / column[:, 8:9]).astype(BF)
    for k in range(8):
        out_ref[k] = result


def finish(*operands):
    return pl.pallas_call(
        finish_kernel,
        out_shape=jax.ShapeDtypeStruct((8, 64, 128), BF),
        in_specs=[SMEM] + [VMEM] * 3,
        out_specs=VMEM,
        scratch_shapes=[pltpu.VMEM((128, 16), F32), pltpu.VMEM((128, 128), F32)],
        cost_estimate=pl.CostEstimate(flops=20_000_000, bytes_accessed=800_000, transcendentals=0),
        compiler_params=pltpu.CompilerParams(vmem_limit_bytes=6 * 1024 * 1024),
        name="finish",
    )(*operands)


def project_kernel(
    place_ref, own_ref, far_ref, w0, w1, w2, w3, keep_ref, gain_ref, out_ref
):
    core = place_ref[0]
    y = place_ref[1]
    x = place_ref[3]
    for k, weight_ref in enumerate((w0, w1, w2, w3)):
        value = jnp.zeros((64, 128), F32)
        for rel, ref in enumerate((own_ref, far_ref)):
            group = core if rel == 0 else 1 - core
            at = pl.ds(pl.multiple_of(group * 1024, 1024), 1024)
            rows = jnp.concatenate([ref[i] for i in range(8)], axis=1)
            value = value + jnp.dot(rows, weight_ref[at, :], preferred_element_type=F32)
        step = lax.rem(x - y - k + 2 * NX, NX)
        out_ref[step] = value.astype(BF)

        @pl.when(step == 0)
        def _():
            rows = pl.ds(pl.multiple_of(2048 + x * 64, 64), 64)
            keep_ref[...] = value + weight_ref[rows, :].astype(F32)
            gain_ref[...] = weight_ref[2304:2320, :]


def project(*operands):
    return pl.pallas_call(
        project_kernel,
        out_shape=(
            jax.ShapeDtypeStruct((64, 128), F32),
            jax.ShapeDtypeStruct((16, 128), BF),
            jax.ShapeDtypeStruct((NX, 64, 128), BF),
        ),
        in_specs=[SMEM] + [VMEM] * 6,
        out_specs=(VMEM,) * 3,
        compiler_params=grant(8),
        cost_estimate=pl.CostEstimate(
            flops=2 * 64 * 2048 * 512, bytes_accessed=2_500_000, transcendentals=0
        ),
        name="project",
    )(*operands)


def middle_kernel(place_ref, keep_ref, r1, r2, r3, gain_ref, mid_ref, out_ref):
    x = place_ref[3]
    mid = keep_ref[...]
    for ref in (r1, r2, r3):
        mid = mid + ref[...].astype(F32)
    mid_ref[...] = mid
    gain = gain_ref[...].astype(F32)[0:1]
    feature = (mid * gain).astype(BF)
    both = jnp.concatenate([mid, mid], axis=0)
    squares = jnp.sum((both * both).T, axis=0, keepdims=True)
    lane = lax.broadcasted_iota(jnp.int32, (1, 128), 1)
    squares = jnp.where(lane // 64 == lax.rem(x, 2), squares, 0.0)
    rows = jnp.concatenate(split_rows(squares) + [jnp.zeros((13, 128), F32)], axis=0).astype(BF)
    for k in range(32):
        out_ref[k, 0:64, :] = feature
        out_ref[k, 64:80, :] = rows


def middle(*operands):
    return pl.pallas_call(
        middle_kernel,
        out_shape=(
            jax.ShapeDtypeStruct((64, 128), F32),
            jax.ShapeDtypeStruct((32, 80, 128), BF),
        ),
        in_specs=[SMEM] + [VMEM] * 5,
        out_specs=(VMEM, VMEM),
        compiler_params=grant(6),
        cost_estimate=pl.CostEstimate(flops=100_000, bytes_accessed=800_000, transcendentals=0),
        name="middle",
    )(*operands)


def gathered(ref, feature):
    pairs = [jnp.zeros((1, 128), F32), jnp.zeros((1, 128), F32)]
    for z in range(NZ):
        for k in range(4):
            feature[k * 64 : k * 64 + 64, z * 128 : z * 128 + 128] = ref[z * 4 + k, 0:64, :]
            stat = ref[z * 4 + k, 64:80, :].astype(F32)
            pairs[k // 2] = pairs[k // 2] + (stat[0:1] + (stat[1:2] + stat[2:3]))
    return jnp.concatenate(pairs, axis=1)


def ffn_product(rel, piece, feature):
    weight = jnp.concatenate([piece[z, rel, 0:224, :] for z in range(NZ)], axis=1)
    return lax.dot_general(weight, feature[...], NT, preferred_element_type=F32)


def ffn_near_kernel(p0, p1, p2, p3, own_ref, square_ref, t0, t1, t2, t3, feature):
    square_ref[...] = jnp.broadcast_to(gathered(own_ref, feature), (8, ROWS))
    for piece, to in ((p0, t0), (p1, t1), (p2, t2), (p3, t3)):
        to[...] = ffn_product(0, piece, feature)


def ffn_far_kernel(
    p0, p1, p2, p3, far_ref, near_ref, t0, t1, t2, t3, keep_ref, square_ref, s1, s2, s3, feature
):
    squares = near_ref[0:1, :] + gathered(far_ref, feature)
    square_ref[...] = jnp.broadcast_to(squares, (8, ROWS))
    rows = jnp.concatenate(split_rows(squares) + [jnp.zeros((13, ROWS), F32)], axis=0).astype(BF)
    for piece, term, to in ((p1, t1, s1), (p2, t2, s2), (p3, t3, s3)):
        to[0:224, :] = (term[...] + ffn_product(1, piece, feature)).astype(BF)
        to[224:240, :] = rows
    keep_ref[...] = t0[...] + ffn_product(1, p0, feature)


def ffn_near(*operands):
    term = jax.ShapeDtypeStruct((224, ROWS), F32)
    return pl.pallas_call(
        ffn_near_kernel,
        out_shape=(jax.ShapeDtypeStruct((8, ROWS), F32), term, term, term, term),
        in_specs=[VMEM] * 5,
        out_specs=(VMEM,) * 5,
        scratch_shapes=[pltpu.VMEM((ROWS, 1024), BF)],
        compiler_params=grant(16),
        cost_estimate=pl.CostEstimate(
            flops=896 * 2048 * 256, bytes_accessed=4_000_000, transcendentals=0
        ),
        name="ffn_near",
    )(*operands)


def ffn_far(*operands):
    sent = jax.ShapeDtypeStruct((240, ROWS), BF)
    return pl.pallas_call(
        ffn_far_kernel,
        out_shape=(
            jax.ShapeDtypeStruct((224, ROWS), F32),
            jax.ShapeDtypeStruct((8, ROWS), F32),
            sent,
            sent,
            sent,
        ),
        in_specs=[VMEM] * 10,
        out_specs=(VMEM,) * 5,
        scratch_shapes=[pltpu.VMEM((ROWS, 1024), BF)],
        compiler_params=grant(16),
        cost_estimate=pl.CostEstimate(
            flops=896 * 2048 * 256, bytes_accessed=4_000_000, transcendentals=0
        ),
        name="ffn_far",
    )(*operands)


def act_kernel(both_ref, square_ref, r1, r2, r3, out_ref):
    both = both_ref[...]
    squares = square_ref[0:1, :]
    for ref in (r1, r2, r3):
        both = both + ref[0:224, :].astype(F32)
        stat = ref[224:240, :].astype(F32)
        squares = squares + (stat[0:1] + (stat[1:2] + stat[2:3]))
    both = both * lax.rsqrt(squares / D + EPS)
    gate = both[0:112]
    out_ref[...] = (gate / (1.0 + jnp.exp(-gate)) * both[112:224]).astype(BF)


def act_of(*operands):
    return pl.pallas_call(
        act_kernel,
        out_shape=jax.ShapeDtypeStruct((112, ROWS), BF),
        in_specs=[VMEM] * 5,
        out_specs=VMEM,
        cost_estimate=pl.CostEstimate(flops=500_000, bytes_accessed=700_000, transcendentals=0),
        compiler_params=pltpu.CompilerParams(vmem_limit_bytes=6 * 1024 * 1024),
        name="act",
    )(*operands)


def down_kernel(rel, p0, p1, p2, p3, a0, a1, a2, a3, *refs):
    act = jnp.concatenate([a0[...], a1[...], a2[...], a3[...]], axis=0)
    weight = jnp.concatenate(
        [
            jnp.concatenate([p[z, rel, 224:336, :] for z in range(NZ)], axis=1)
            for p in (p0, p1, p2, p3)
        ],
        axis=0,
    )
    term = lax.dot_general(act, weight, TN, preferred_element_type=F32)
    for z in range(NZ):
        block = term[:, z * 128 : z * 128 + 128]
        if rel == 1:
            refs[-1][z] = block.astype(BF)
        else:
            block = (block + refs[0][z].astype(F32)).astype(BF)
            for k in range(NX):
                refs[-1][z * NX + k, 0:64, :] = block[k * 64 : k * 64 + 64, :]
                refs[-1][z * NX + k, 64:128, :] = refs[1][z * NX + k]


def down(rel, *operands):
    return pl.pallas_call(
        functools.partial(down_kernel, rel),
        out_shape=jax.ShapeDtypeStruct((NZ, ROWS, 128) if rel else (32, 128, 128), BF),
        in_specs=[VMEM] * len(operands),
        out_specs=VMEM,
        compiler_params=pltpu.CompilerParams(vmem_limit_bytes=16 * 1024 * 1024),
        cost_estimate=pl.CostEstimate(
            flops=448 * 2048 * 256, bytes_accessed=4_000_000, transcendentals=0
        ),
        name="down",
    )(*operands)


def shards(
    hidden_rows,
    cache_kv,
    sel_index,
    doc_order,
    attn_gain,
    w_query,
    w_keyval,
    w_output,
    ffn_gain,
    w_in,
    w_out,
):
    z, x, c, y = (lax.axis_index(name) for name in ("z", "x", "c", "y"))
    mine = (z * NX + x) * NC + c
    other = 1 - c

    def half(group):
        return jnp.concatenate(
            [
                lax.dynamic_slice_in_dim(w_query, group * 1024, 1024, 1),
                lax.dynamic_slice_in_dim(w_keyval[:, 0], group * 128, 128, 1),
                lax.dynamic_slice_in_dim(w_keyval[:, 1], group * 128, 128, 1),
            ],
            axis=1,
        )

    place = jnp.stack([c, y, z, x]).astype(jnp.int32)

    message = jnp.concatenate(
        [hidden_rows, jnp.broadcast_to(attn_gain[None, :], (16, 128))], axis=0
    )
    theirs = exchange_cores(message)
    weight_theirs = exchange_cores(half(other))

    theirs, raw = hold(theirs, cache_kv)
    cache = raw.reshape(DOC_LEN, 512)

    weight = jnp.concatenate([half(c), weight_theirs], axis=0)
    inputs = jnp.concatenate([hidden_rows, theirs[:ROWS]], axis=1).astype(F32)
    gain = jnp.concatenate([attn_gain, theirs[ROWS]], axis=0).astype(F32)
    squares = jnp.sum(inputs * inputs, axis=1)
    scaled = (inputs * gain[None, :]).astype(BF)
    partial = jnp.dot(scaled, weight, preferred_element_type=F32).astype(BF)
    query_part = jnp.transpose(partial[:, :1024].reshape(4, 64, 8, 128), (2, 0, 1, 3))
    new_part = jnp.transpose(partial[:, 1024:].reshape(8, 32, 2, 128), (0, 2, 1, 3))
    square_parts = jnp.stack(parts_of(squares) + [jnp.zeros((ROWS,), BF)] * 5)
    by_x = jnp.transpose(square_parts.reshape(8, 4, 64), (1, 0, 2))
    by_z = jnp.transpose(square_parts.reshape(8, 8, 32), (1, 0, 2))
    square_parts = jnp.concatenate(
        [
            jnp.broadcast_to(by_x[None], (8, 4, 8, 64)),
            jnp.broadcast_to(by_z[:, None], (8, 4, 8, 32)),
            jnp.zeros((8, 4, 8, 32), BF),
        ],
        axis=3,
    )
    new_part = jnp.broadcast_to(new_part.reshape(8, 1, 64, 128), (8, 4, 64, 128))
    payload = jnp.concatenate([query_part, new_part, square_parts], axis=2).reshape(32, 136, 128)

    payload, cache, sel_index, doc_order = hold(payload, cache, sel_index, doc_order)
    reordered = cache.reshape(POOL, 8, 512).at[doc_order].get(mode="promise_in_bounds")
    reordered = reordered.reshape(32, 2, 8, 512)
    stay = lax.dynamic_index_in_dim(reordered, c, 1, keepdims=False)
    leave = lax.dynamic_index_in_dim(reordered, other, 1, keepdims=False)
    come, w_in, w_out = hold(exchange_cores(leave), w_in, w_out)
    right, left, across = shift_x(cache, 1), shift_x(cache, -1), shift_x(cache, 2)
    arrived, right, left, across = hold(swap_zx(payload), right, left, across)
    piece = scale(arrived)

    flat_in = jnp.transpose(w_in, (1, 2, 0)).reshape(224, D)
    pieces = weight_slices(place, flat_in, w_out)
    slices = [pieces[0], shift_y(pieces[1], 1), None, shift_y(pieces[3], 3)]

    w_output = jnp.concatenate(
        [w_output, hidden_rows, jnp.broadcast_to(ffn_gain[None, :], (16, 128))], axis=0
    )

    slot_of_doc, row_pos = positions(sel_index, doc_order)
    my_pos = lax.dynamic_slice_in_dim(row_pos, x * 64, 64, 0)
    my_pos = jnp.concatenate([my_pos, my_pos])[None, :]
    token = jnp.arange(8, dtype=jnp.int32)
    docs = jnp.arange(POOL, dtype=jnp.int32)
    key_pos = []
    for step in (0, 1, 3, 2):
        base = ((z * NX + (x - step) % NX) * NC + c) * 8
        name = (docs[:, None] * DOC_LEN + base + token[None, :]).reshape(DOC_LEN)
        at = (slot_of_doc[:, None] * DOC_LEN + base + token[None, :]).reshape(DOC_LEN)
        written = jnp.any(name[:, None] == sel_index[None, :], axis=1)
        key_pos.append(jnp.where(written, DOC_LEN * POOL * 2, at))
    bias = jnp.where(jnp.concatenate(key_pos)[:, None] <= my_pos, 0.0, NEG).astype(BF)
    new_bias = jnp.where(row_pos[:, None] <= my_pos, 0.0, NEG).astype(BF)

    piece, bias, new_bias, pieces, w_output = hold(piece, bias, new_bias, pieces, w_output)
    own = swap_z(piece)
    wo_right, wo_left = shift_x(w_output, 1), shift_x(w_output, -1)
    others = exchange_cores(own)
    acc, acc_sent, stats = attend(place, bias, own, others, (cache, right, left, across))

    payload = merge(acc, stats, exchange_cores(acc_sent))
    payload, w_output, wo_right, wo_left, stay, come, slices[1], slices[3], last = hold(
        payload, w_output, wo_right, wo_left, stay, come, slices[1], slices[3], pieces[2]
    )
    wo_all = [w_output, wo_right, shift_x(w_output, 2), wo_left]
    slices[2] = shift_y(last, 2)
    arrived = swap_z(payload)

    piece = finish(place, arrived, own, new_bias)
    attended = swap_z(piece)
    attended_theirs = exchange_cores(attended)

    keep, gain, chunks = project(place, attended, attended_theirs, *wo_all)
    keep, chunks, slices[2] = hold(keep, chunks, slices[2])
    got = [shift_y(chunks[step], step) for step in range(1, 4)]
    mid, payload = middle(place, keep, *got, gain)
    payload, stay, come = hold(payload, stay, come)

    lower = jnp.where(c == 0, stay, come)
    upper = jnp.where(c == 0, come, stay)
    cache_out = jnp.concatenate([lower, upper], axis=1).reshape(32, 16, 4, 128)
    cache_out = jnp.transpose(cache_out, (0, 2, 1, 3)).reshape(32, 64, 128)
    arrived, cache_out = hold(swap_zx(payload), cache_out)
    arrived_theirs = exchange_cores(arrived)

    both, squares, *sent = ffn_far(*slices, arrived_theirs, *ffn_near(*slices, arrived))
    got = [shift_y(sent[step - 1], -step) for step in range(1, 4)]
    act = act_of(both, squares, *got)
    acts = [act] + [shift_y(act, step) for step in range(1, 4)]
    got = exchange_cores(down(1, *slices, *acts))
    arrived = swap_zx(down(0, *slices, *acts, got, cache_out))
    summed = jnp.sum(arrived[:, :64].astype(F32), axis=0)
    slot_cache = jnp.transpose(arrived[:, 64:].reshape(32, 4, 16, 128), (0, 2, 1, 3))

    sel_key = jnp.where(row_pos // DOC_LEN == mine, row_pos % DOC_LEN, -1)
    hits = sel_key[None, :] == jnp.arange(DOC_LEN, dtype=jnp.int32)[:, None]
    covered = jnp.any(hits, axis=1)
    new_own, new_others = own[:, 64:], others[:, 64:]
    new_flat = jnp.stack(
        [jnp.where(c == 0, new_own, new_others), jnp.where(c == 0, new_others, new_own)]
    ).reshape(2, 8, 2, 32, 128)
    new_flat = jnp.transpose(new_flat, (1, 3, 2, 0, 4)).reshape(ROWS, 512)
    placed = jnp.dot(hits.astype(BF), new_flat, preferred_element_type=F32).astype(BF)
    joined = jnp.where(covered[:, None], placed, slot_cache.reshape(DOC_LEN, 512))
    joined = joined.reshape(DOC_LEN, 2, 256)
    result = permute_xy((mid + summed).astype(BF), lambda a, b: (b, a))
    return (result, joined)


def solution(mesh):
    split = Mesh(mesh.devices.reshape(NZ, NX, NC, NY), ("z", "x", "c", "y"))
    pool = ("z", "x", "c")
    return jax.shard_map(
        shards,
        mesh=split,
        in_specs=(
            P(None, pool),
            P(None, pool, None, "y"),
            P(),
            P(),
            P(pool),
            P(pool, "y"),
            P(pool, None, "y"),
            P("y", pool),
            P(pool),
            P(None, None, ("z", "x", "c", "y")),
            P(("z", "x", "c", "y"), None),
        ),
        out_specs=(P("y", pool), P(pool, None, "y")),
        check_vma=False,
    )
```

```python
import functools

import jax
import jax.numpy as jnp
from jax import lax
from jax.experimental import pallas as pl
from jax.experimental.pallas import tpu as pltpu
from jax.sharding import Mesh
from jax.sharding import PartitionSpec as P

D = 8192
HEAD_DIM = 128
DOC_LEN = 512
SEL_DEV = 3
EPS = 1e-05
NEG = -1e30
FLOOR = -1e29
NZ, NX, NC, NY = 8, 4, 2, 4
POOL = NZ * NX * NC
ROWS = 256

BF = jnp.bfloat16
F32 = jnp.float32


def exchange_cores(value):
    return lax.ppermute(value, "c", [(0, 1), (1, 0)])


def shift_y(value, step):
    return lax.ppermute(value, "y", [(i, (i + step) % NY) for i in range(NY)])


def permute_xy(value, target):
    pairs = []
    for x in range(NX):
        for y in range(NY):
            to_x, to_y = target(x, y)
            pairs.append((x * NY + y, (to_x % NX) * NY + to_y % NY))
    return lax.ppermute(value, ("x", "y"), pairs)


def swap_zx(value):
    return lax.all_to_all(value, ("z", "x"), 0, 0, tiled=True)


def parts_of(value):
    high = lax.reduce_precision(value, 8, 7)
    rest = value - high
    middle = lax.reduce_precision(rest, 8, 7)
    low = rest - middle
    return [high.astype(BF), middle.astype(BF), low.astype(BF)]


def shift_x(value, step):
    return lax.ppermute(value, "x", [(i, (i + step) % NX) for i in range(NX)])


def swap_z(value):
    return lax.all_to_all(value, "z", 0, 0, tiled=True)


def hold(*values):
    return lax.optimization_barrier(values)


def positions(sel_index, doc_order):
    docs = jnp.arange(POOL, dtype=jnp.int32)
    slot_of_doc = jnp.sum(jnp.where(doc_order[:, None] == docs[None, :], docs[:, None], 0), axis=0)
    sel_doc = sel_index // DOC_LEN
    sel_tok = sel_index % DOC_LEN
    sel_slot = jnp.sum(
        jnp.where(sel_doc[:, None] == docs[None, :], slot_of_doc[None, :], 0), axis=1
    )
    sel_pos = sel_slot * DOC_LEN + sel_tok
    query_pos = DOC_LEN * POOL + docs
    row_pos = jnp.concatenate(
        [sel_pos.reshape(POOL, SEL_DEV), query_pos[:, None]], axis=1
    ).reshape(ROWS)
    return slot_of_doc, row_pos


def slices_kernel(place_ref, in_ref, out_ref, *pieces):
    core = place_ref[0]
    y = place_ref[1]
    for step in range(4):
        base = lax.rem(y + step, NY) * 256
        for rel in range(2):
            group = core if rel == 0 else 1 - core
            lanes = pl.ds(pl.multiple_of(base + group * 128, 128), 128)
            pieces[step][0, rel, 0:224, :] = in_ref[:, lanes]
            pieces[step][0, rel, 224:336, :] = out_ref[:, lanes]


def weight_slices(place, flat_in, w_out):
    return pl.pallas_call(
        slices_kernel,
        grid=(NZ,),
        out_shape=tuple(jax.ShapeDtypeStruct((NZ, 2, 336, 128), BF) for _ in range(4)),
        in_specs=[
            pl.BlockSpec(memory_space=pltpu.SMEM),
            pl.BlockSpec((224, 1024), lambda k: (0, k)),
            pl.BlockSpec((112, 1024), lambda k: (0, k)),
        ],
        out_specs=tuple(pl.BlockSpec((1, 2, 336, 128), lambda k: (k, 0, 0, 0)) for _ in range(4)),
        compiler_params=pltpu.CompilerParams(vmem_limit_bytes=8 * 1024 * 1024),
        cost_estimate=pl.CostEstimate(flops=0, bytes_accessed=11_000_000, transcendentals=0),
        name="weight_slices",
    )(place, flat_in, w_out)


NT = (((1,), (1,)), ((), ()))
TN = (((0,), (0,)), ((), ()))


def split_rows(value):
    high = value.astype(BF).astype(F32)
    rest = value - high
    middle = rest.astype(BF).astype(F32)
    return [high, middle, rest - middle]


VMEM = pl.BlockSpec(memory_space=pltpu.VMEM)
SMEM = pl.BlockSpec(memory_space=pltpu.SMEM)


def grant(mib):
    return pltpu.CompilerParams(vmem_limit_bytes=mib * 1024 * 1024)


def scale_kernel(in_ref, out_ref):
    value = in_ref[0].astype(F32)
    for k in range(1, 32):
        value = value + in_ref[k].astype(F32)
    squares = value[128:129] + (value[129:130] + value[130:131])
    factor = jnp.broadcast_to(lax.rsqrt(squares / D + EPS), (8, 128)).T
    by_x = factor[0:64, 0:1]
    by_z = factor[64:96, 0:1]
    result = jnp.concatenate(
        [value[0:64] * by_x, value[64:96] * by_z, value[96:128] * by_z], axis=0
    ).astype(BF)
    for k in range(NZ):
        out_ref[k] = result


def scale(value):
    return pl.pallas_call(
        scale_kernel,
        out_shape=jax.ShapeDtypeStruct((NZ, 128, 128), BF),
        in_specs=[VMEM],
        out_specs=VMEM,
        compiler_params=grant(6),
        cost_estimate=pl.CostEstimate(flops=600_000, bytes_accessed=1_500_000, transcendentals=0),
        name="scale",
    )(value)


def attend_kernel(
    place_ref, bias_ref, own_ref, other_ref, c0, c1, c2, c3, acc_ref, sent_ref, stat_ref
):
    core = place_ref[0]
    blocks = (c0, c1, c2, c3)
    for rel in range(2):
        query_ref = own_ref if rel == 0 else other_ref
        group = core if rel == 0 else 1 - core
        key_at = pl.ds(pl.multiple_of(group * 128, 128), 128)
        value_at = pl.ds(pl.multiple_of(256 + group * 128, 128), 128)
        for half in range(2):
            lanes = slice(half * 256, half * 256 + 256)
            query = jnp.concatenate(
                [query_ref[half * 4 + i, 0:64, :] for i in range(4)], axis=0
            )
            scores = []
            top = jnp.full((1, 256), FLOOR, F32)
            for k in range(4):
                bias = bias_ref[k * 512 : k * 512 + 512, :].astype(F32)
                part = lax.dot_general(
                    blocks[k][:, key_at], query, NT, preferred_element_type=F32
                ) * (HEAD_DIM**-0.5) + jnp.concatenate([bias, bias], axis=1)
                scores.append(part)
                top = jnp.maximum(top, jnp.max(part, axis=0, keepdims=True))
            total = jnp.zeros((1, 256), F32)
            acc = jnp.zeros((128, 256), F32)
            for k in range(4):
                probs = jnp.exp(scores[k] - top)
                total = total + jnp.sum(probs, axis=0, keepdims=True)
                acc = acc + lax.dot_general(
                    blocks[k][:, value_at], probs.astype(BF), TN, preferred_element_type=F32
                )
            if rel == 0:
                acc_ref[:, lanes] = acc
                stat_ref[0:1, lanes] = top
                stat_ref[1:2, lanes] = total
            else:
                stats = split_rows(top) + split_rows(total) + [jnp.zeros((10, 256), F32)]
                sent_ref[0:128, lanes] = acc.astype(BF)
                sent_ref[128:144, lanes] = jnp.concatenate(stats, axis=0).astype(BF)


def attend(place, bias, own, other, blocks):
    vmem = pl.BlockSpec(memory_space=pltpu.VMEM)
    return pl.pallas_call(
        attend_kernel,
        out_shape=(
            jax.ShapeDtypeStruct((128, 512), F32),
            jax.ShapeDtypeStruct((144, 512), BF),
            jax.ShapeDtypeStruct((8, 512), F32),
        ),
        in_specs=[pl.BlockSpec(memory_space=pltpu.SMEM)] + [vmem] * 7,
        out_specs=(vmem, vmem, vmem),
        compiler_params=pltpu.CompilerParams(vmem_limit_bytes=16 * 1024 * 1024),
        cost_estimate=pl.CostEstimate(
            flops=2 * 16 * 2 * 2048 * 128 * 64, bytes_accessed=6_000_000, transcendentals=2097152
        ),
        name="attend",
    )(place, bias, own, other, *blocks)


def merge_kernel(acc_ref, stat_ref, far_ref, out_ref):
    near_top = stat_ref[0:1, :]
    stat = far_ref[128:144, :].astype(F32)
    far_top = stat[0:1] + (stat[1:2] + stat[2:3])
    far_total = stat[3:4] + (stat[4:5] + stat[5:6])
    top = jnp.maximum(near_top, far_top)
    near = jnp.exp(near_top - top)
    far = jnp.exp(far_top - top)
    total = stat_ref[1:2, :] * near + far_total * far
    acc = acc_ref[...] * near + far_ref[0:128, :].astype(F32) * far
    rows = acc.T.astype(BF)
    stats = split_rows(top) + split_rows(total) + [jnp.zeros((10, 512), F32)]
    stats = jnp.concatenate(stats, axis=0).astype(BF)
    for head in range(8):
        pair = head // 2
        out_ref[head, 0:64, :] = rows[head * 64 : head * 64 + 64, :]
        out_ref[head, 64:80, :] = stats[:, pair * 128 : pair * 128 + 128]


def merge(*operands):
    return pl.pallas_call(
        merge_kernel,
        out_shape=jax.ShapeDtypeStruct((8, 80, 128), BF),
        in_specs=[VMEM] * 3,
        out_specs=VMEM,
        cost_estimate=pl.CostEstimate(flops=500_000, bytes_accessed=1_000_000, transcendentals=0),
        compiler_params=pltpu.CompilerParams(vmem_limit_bytes=6 * 1024 * 1024),
        name="merge",
    )(*operands)


def finish_kernel(
    place_ref, arrived_ref, own_ref, bias_ref, out_ref, column_ref, new_ref
):
    z = place_ref[2]
    keys = jnp.concatenate([own_ref[k, 64:96, :] for k in range(8)], axis=0)
    values = jnp.concatenate([own_ref[k, 96:128, :] for k in range(8)], axis=0)
    query = own_ref[z, 0:64, :]
    query = jnp.concatenate([query, query], axis=0)
    scores = lax.dot_general(keys, query, NT, preferred_element_type=F32)
    scores = scores * (HEAD_DIM**-0.5) + bias_ref[...].astype(F32)
    tops = []
    sums = []
    for k in range(8):
        stat = arrived_ref[k, 64:80, :].astype(F32)
        tops.append(stat[0:1] + (stat[1:2] + stat[2:3]))
        sums.append(stat[3:4] + (stat[4:5] + stat[5:6]))
    tops = jnp.concatenate(tops, axis=0)
    sums = jnp.concatenate(sums, axis=0)
    top = jnp.maximum(
        jnp.max(tops, axis=0, keepdims=True), jnp.max(scores, axis=0, keepdims=True)
    )
    by = jnp.exp(tops - top)
    probs = jnp.exp(scores - top)
    norm = jnp.sum(sums * by, axis=0, keepdims=True) + jnp.sum(probs, axis=0, keepdims=True)
    column_ref[...] = jnp.concatenate([by, jnp.broadcast_to(norm, (8, 128))], axis=0).T
    new_ref[...] = lax.dot_general(
        probs.astype(BF), values, TN, preferred_element_type=F32
    )
    mine = pl.ds(pl.multiple_of(lax.rem(z, 2) * 64, 64), 64)
    column = column_ref[mine, :]
    acc = new_ref[mine, :]
    for k in range(8):
        acc = acc + arrived_ref[k, 0:64, :].astype(F32) * column[:, k : k + 1]
    result = (acc / column[:, 8:9]).astype(BF)
    for k in range(8):
        out_ref[k] = result


def finish(*operands):
    return pl.pallas_call(
        finish_kernel,
        out_shape=jax.ShapeDtypeStruct((8, 64, 128), BF),
        in_specs=[SMEM] + [VMEM] * 3,
        out_specs=VMEM,
        scratch_shapes=[pltpu.VMEM((128, 16), F32), pltpu.VMEM((128, 128), F32)],
        cost_estimate=pl.CostEstimate(flops=20_000_000, bytes_accessed=800_000, transcendentals=0),
        compiler_params=pltpu.CompilerParams(vmem_limit_bytes=6 * 1024 * 1024),
        name="finish",
    )(*operands)


def project_kernel(
    place_ref, own_ref, far_ref, w0, w1, w2, w3, keep_ref, gain_ref, out_ref
):
    core = place_ref[0]
    y = place_ref[1]
    x = place_ref[3]
    for k, weight_ref in enumerate((w0, w1, w2, w3)):
        value = jnp.zeros((64, 128), F32)
        for rel, ref in enumerate((own_ref, far_ref)):
            group = core if rel == 0 else 1 - core
            at = pl.ds(pl.multiple_of(group * 1024, 1024), 1024)
            rows = jnp.concatenate([ref[i] for i in range(8)], axis=1)
            value = value + jnp.dot(rows, weight_ref[at, :], preferred_element_type=F32)
        step = lax.rem(x - y - k + 2 * NX, NX)
        out_ref[step] = value.astype(BF)

        @pl.when(step == 0)
        def _():
            rows = pl.ds(pl.multiple_of(2048 + x * 64, 64), 64)
            keep_ref[...] = value + weight_ref[rows, :].astype(F32)
            gain_ref[...] = weight_ref[2304:2320, :]


def project(*operands):
    return pl.pallas_call(
        project_kernel,
        out_shape=(
            jax.ShapeDtypeStruct((64, 128), F32),
            jax.ShapeDtypeStruct((16, 128), BF),
            jax.ShapeDtypeStruct((NX, 64, 128), BF),
        ),
        in_specs=[SMEM] + [VMEM] * 6,
        out_specs=(VMEM,) * 3,
        compiler_params=grant(8),
        cost_estimate=pl.CostEstimate(
            flops=2 * 64 * 2048 * 512, bytes_accessed=2_500_000, transcendentals=0
        ),
        name="project",
    )(*operands)


def middle_kernel(place_ref, keep_ref, r1, r2, r3, gain_ref, mid_ref, out_ref):
    x = place_ref[3]
    mid = keep_ref[...]
    for ref in (r1, r2, r3):
        mid = mid + ref[...].astype(F32)
    mid_ref[...] = mid
    gain = gain_ref[...].astype(F32)[0:1]
    feature = (mid * gain).astype(BF)
    both = jnp.concatenate([mid, mid], axis=0)
    squares = jnp.sum((both * both).T, axis=0, keepdims=True)
    lane = lax.broadcasted_iota(jnp.int32, (1, 128), 1)
    squares = jnp.where(lane // 64 == lax.rem(x, 2), squares, 0.0)
    rows = jnp.concatenate(split_rows(squares) + [jnp.zeros((13, 128), F32)], axis=0).astype(BF)
    for k in range(32):
        out_ref[k, 0:64, :] = feature
        out_ref[k, 64:80, :] = rows


def middle(*operands):
    return pl.pallas_call(
        middle_kernel,
        out_shape=(
            jax.ShapeDtypeStruct((64, 128), F32),
            jax.ShapeDtypeStruct((32, 80, 128), BF),
        ),
        in_specs=[SMEM] + [VMEM] * 5,
        out_specs=(VMEM, VMEM),
        compiler_params=grant(6),
        cost_estimate=pl.CostEstimate(flops=100_000, bytes_accessed=800_000, transcendentals=0),
        name="middle",
    )(*operands)


def gathered(ref, feature):
    pairs = [jnp.zeros((1, 128), F32), jnp.zeros((1, 128), F32)]
    for z in range(NZ):
        for k in range(4):
            feature[k * 64 : k * 64 + 64, z * 128 : z * 128 + 128] = ref[z * 4 + k, 0:64, :]
            stat = ref[z * 4 + k, 64:80, :].astype(F32)
            pairs[k // 2] = pairs[k // 2] + (stat[0:1] + (stat[1:2] + stat[2:3]))
    return jnp.concatenate(pairs, axis=1)


def ffn_product(rel, piece, feature):
    weight = jnp.concatenate([piece[z, rel, 0:224, :] for z in range(NZ)], axis=1)
    return lax.dot_general(weight, feature[...], NT, preferred_element_type=F32)


def ffn_near_kernel(p0, p1, p2, p3, own_ref, square_ref, t0, t1, t2, t3, feature):
    square_ref[...] = jnp.broadcast_to(gathered(own_ref, feature), (8, ROWS))
    for piece, to in ((p0, t0), (p1, t1), (p2, t2), (p3, t3)):
        to[...] = ffn_product(0, piece, feature)


def ffn_far_kernel(
    p0, p1, p2, p3, far_ref, near_ref, t0, t1, t2, t3, keep_ref, square_ref, s1, s2, s3, feature
):
    squares = near_ref[0:1, :] + gathered(far_ref, feature)
    square_ref[...] = jnp.broadcast_to(squares, (8, ROWS))
    rows = jnp.concatenate(split_rows(squares) + [jnp.zeros((13, ROWS), F32)], axis=0).astype(BF)
    for piece, term, to in ((p1, t1, s1), (p2, t2, s2), (p3, t3, s3)):
        to[0:224, :] = (term[...] + ffn_product(1, piece, feature)).astype(BF)
        to[224:240, :] = rows
    keep_ref[...] = t0[...] + ffn_product(1, p0, feature)


def ffn_near(*operands):
    term = jax.ShapeDtypeStruct((224, ROWS), F32)
    return pl.pallas_call(
        ffn_near_kernel,
        out_shape=(jax.ShapeDtypeStruct((8, ROWS), F32), term, term, term, term),
        in_specs=[VMEM] * 5,
        out_specs=(VMEM,) * 5,
        scratch_shapes=[pltpu.VMEM((ROWS, 1024), BF)],
        compiler_params=grant(16),
        cost_estimate=pl.CostEstimate(
            flops=896 * 2048 * 256, bytes_accessed=4_000_000, transcendentals=0
        ),
        name="ffn_near",
    )(*operands)


def ffn_far(*operands):
    sent = jax.ShapeDtypeStruct((240, ROWS), BF)
    return pl.pallas_call(
        ffn_far_kernel,
        out_shape=(
            jax.ShapeDtypeStruct((224, ROWS), F32),
            jax.ShapeDtypeStruct((8, ROWS), F32),
            sent,
            sent,
            sent,
        ),
        in_specs=[VMEM] * 10,
        out_specs=(VMEM,) * 5,
        scratch_shapes=[pltpu.VMEM((ROWS, 1024), BF)],
        compiler_params=grant(16),
        cost_estimate=pl.CostEstimate(
            flops=896 * 2048 * 256, bytes_accessed=4_000_000, transcendentals=0
        ),
        name="ffn_far",
    )(*operands)


def act_kernel(both_ref, square_ref, r1, r2, r3, out_ref):
    both = both_ref[...]
    squares = square_ref[0:1, :]
    for ref in (r1, r2, r3):
        both = both + ref[0:224, :].astype(F32)
        stat = ref[224:240, :].astype(F32)
        squares = squares + (stat[0:1] + (stat[1:2] + stat[2:3]))
    both = both * lax.rsqrt(squares / D + EPS)
    gate = both[0:112]
    out_ref[...] = (gate / (1.0 + jnp.exp(-gate)) * both[112:224]).astype(BF)


def act_of(*operands):
    return pl.pallas_call(
        act_kernel,
        out_shape=jax.ShapeDtypeStruct((112, ROWS), BF),
        in_specs=[VMEM] * 5,
        out_specs=VMEM,
        cost_estimate=pl.CostEstimate(flops=500_000, bytes_accessed=700_000, transcendentals=0),
        compiler_params=pltpu.CompilerParams(vmem_limit_bytes=6 * 1024 * 1024),
        name="act",
    )(*operands)


def down_kernel(rel, p0, p1, p2, p3, a0, a1, a2, a3, *refs):
    act = jnp.concatenate([a0[...], a1[...], a2[...], a3[...]], axis=0)
    weight = jnp.concatenate(
        [
            jnp.concatenate([p[z, rel, 224:336, :] for z in range(NZ)], axis=1)
            for p in (p0, p1, p2, p3)
        ],
        axis=0,
    )
    term = lax.dot_general(act, weight, TN, preferred_element_type=F32)
    for z in range(NZ):
        block = term[:, z * 128 : z * 128 + 128]
        if rel == 1:
            refs[-1][z] = block.astype(BF)
        else:
            block = (block + refs[0][z].astype(F32)).astype(BF)
            for k in range(NX):
                refs[-1][z * NX + k, 0:64, :] = block[k * 64 : k * 64 + 64, :]
                refs[-1][z * NX + k, 64:128, :] = refs[1][z * NX + k]


def down(rel, *operands):
    return pl.pallas_call(
        functools.partial(down_kernel, rel),
        out_shape=jax.ShapeDtypeStruct((NZ, ROWS, 128) if rel else (32, 128, 128), BF),
        in_specs=[VMEM] * len(operands),
        out_specs=VMEM,
        compiler_params=pltpu.CompilerParams(vmem_limit_bytes=16 * 1024 * 1024),
        cost_estimate=pl.CostEstimate(
            flops=448 * 2048 * 256, bytes_accessed=4_000_000, transcendentals=0
        ),
        name="down",
    )(*operands)


def shards(
    hidden_rows,
    cache_kv,
    sel_index,
    doc_order,
    attn_gain,
    w_query,
    w_keyval,
    w_output,
    ffn_gain,
    w_in,
    w_out,
):
    z, x, c, y = (lax.axis_index(name) for name in ("z", "x", "c", "y"))
    mine = (z * NX + x) * NC + c
    other = 1 - c

    def half(group):
        return jnp.concatenate(
            [
                lax.dynamic_slice_in_dim(w_query, group * 1024, 1024, 1),
                lax.dynamic_slice_in_dim(w_keyval[:, 0], group * 128, 128, 1),
                lax.dynamic_slice_in_dim(w_keyval[:, 1], group * 128, 128, 1),
            ],
            axis=1,
        )

    place = jnp.stack([c, y, z, x]).astype(jnp.int32)

    theirs = exchange_cores(hidden_rows)
    gain_theirs = exchange_cores(attn_gain.reshape(1, 128))
    weight_theirs = exchange_cores(half(other))

    theirs, raw = hold(theirs, cache_kv)
    cache = raw.reshape(DOC_LEN, 512)

    weight = jnp.concatenate([half(c), weight_theirs], axis=0)
    inputs = jnp.concatenate([hidden_rows, theirs], axis=1).astype(F32)
    gain = jnp.concatenate([attn_gain, gain_theirs[0]], axis=0).astype(F32)
    squares = jnp.sum(inputs * inputs, axis=1)
    scaled = (inputs * gain[None, :]).astype(BF)
    partial = jnp.dot(scaled, weight, preferred_element_type=F32).astype(BF)
    query_part = jnp.transpose(partial[:, :1024].reshape(4, 64, 8, 128), (2, 0, 1, 3))
    new_part = jnp.transpose(partial[:, 1024:].reshape(8, 32, 2, 128), (0, 2, 1, 3))
    square_parts = jnp.stack(parts_of(squares) + [jnp.zeros((ROWS,), BF)] * 5)
    by_x = jnp.transpose(square_parts.reshape(8, 4, 64), (1, 0, 2))
    by_z = jnp.transpose(square_parts.reshape(8, 8, 32), (1, 0, 2))
    square_parts = jnp.concatenate(
        [
            jnp.broadcast_to(by_x[None], (8, 4, 8, 64)),
            jnp.broadcast_to(by_z[:, None], (8, 4, 8, 32)),
            jnp.zeros((8, 4, 8, 32), BF),
        ],
        axis=3,
    )
    new_part = jnp.broadcast_to(new_part.reshape(8, 1, 64, 128), (8, 4, 64, 128))
    payload = jnp.concatenate([query_part, new_part, square_parts], axis=2).reshape(32, 136, 128)

    payload, cache, sel_index, doc_order = hold(payload, cache, sel_index, doc_order)
    reordered = cache.reshape(POOL, 8, 512).at[doc_order].get(mode="promise_in_bounds")
    reordered = reordered.reshape(32, 2, 8, 512)
    stay = lax.dynamic_index_in_dim(reordered, c, 1, keepdims=False)
    leave = lax.dynamic_index_in_dim(reordered, other, 1, keepdims=False)
    come, w_in, w_out = hold(exchange_cores(leave), w_in, w_out)
    right, left, across = shift_x(cache, 1), shift_x(cache, -1), shift_x(cache, 2)
    arrived, right, left, across = hold(swap_zx(payload), right, left, across)
    piece = scale(arrived)

    flat_in = jnp.transpose(w_in, (1, 2, 0)).reshape(224, D)
    pieces = weight_slices(place, flat_in, w_out)
    slices = [pieces[0], shift_y(pieces[1], 1), None, shift_y(pieces[3], 3)]

    w_output = jnp.concatenate(
        [w_output, hidden_rows, jnp.broadcast_to(ffn_gain[None, :], (16, 128))], axis=0
    )

    slot_of_doc, row_pos = positions(sel_index, doc_order)
    my_pos = lax.dynamic_slice_in_dim(row_pos, x * 64, 64, 0)
    my_pos = jnp.concatenate([my_pos, my_pos])[None, :]
    token = jnp.arange(8, dtype=jnp.int32)
    docs = jnp.arange(POOL, dtype=jnp.int32)
    key_pos = []
    for step in (0, 1, 3, 2):
        base = ((z * NX + (x - step) % NX) * NC + c) * 8
        name = (docs[:, None] * DOC_LEN + base + token[None, :]).reshape(DOC_LEN)
        at = (slot_of_doc[:, None] * DOC_LEN + base + token[None, :]).reshape(DOC_LEN)
        written = jnp.any(name[:, None] == sel_index[None, :], axis=1)
        key_pos.append(jnp.where(written, DOC_LEN * POOL * 2, at))
    bias = jnp.where(jnp.concatenate(key_pos)[:, None] <= my_pos, 0.0, NEG).astype(BF)
    new_bias = jnp.where(row_pos[:, None] <= my_pos, 0.0, NEG).astype(BF)

    piece, bias, new_bias, pieces, w_output = hold(piece, bias, new_bias, pieces, w_output)
    own = swap_z(piece)
    wo_right, wo_left = shift_x(w_output, 1), shift_x(w_output, -1)
    others = exchange_cores(own)
    acc, acc_sent, stats = attend(place, bias, own, others, (cache, right, left, across))

    payload = merge(acc, stats, exchange_cores(acc_sent))
    payload, w_output, wo_right, wo_left, stay, come, slices[1], slices[3], last = hold(
        payload, w_output, wo_right, wo_left, stay, come, slices[1], slices[3], pieces[2]
    )
    wo_all = [w_output, wo_right, shift_x(w_output, 2), wo_left]
    slices[2] = shift_y(last, 2)
    arrived = swap_z(payload)

    piece = finish(place, arrived, own, new_bias)
    attended = swap_z(piece)
    attended_theirs = exchange_cores(attended)

    keep, gain, chunks = project(place, attended, attended_theirs, *wo_all)
    keep, chunks, slices[2] = hold(keep, chunks, slices[2])
    got = [shift_y(chunks[step], step) for step in range(1, 4)]
    mid, payload = middle(place, keep, *got, gain)
    payload, stay, come = hold(payload, stay, come)

    lower = jnp.where(c == 0, stay, come)
    upper = jnp.where(c == 0, come, stay)
    cache_out = jnp.concatenate([lower, upper], axis=1).reshape(32, 16, 4, 128)
    cache_out = jnp.transpose(cache_out, (0, 2, 1, 3)).reshape(32, 64, 128)
    arrived, cache_out = hold(swap_zx(payload), cache_out)
    arrived_theirs = exchange_cores(arrived)

    both, squares, *sent = ffn_far(*slices, arrived_theirs, *ffn_near(*slices, arrived))
    got = [shift_y(sent[step - 1], -step) for step in range(1, 4)]
    act = act_of(both, squares, *got)
    acts = [act] + [shift_y(act, step) for step in range(1, 4)]
    got = exchange_cores(down(1, *slices, *acts))
    arrived = swap_zx(down(0, *slices, *acts, got, cache_out))
    summed = jnp.sum(arrived[:, :64].astype(F32), axis=0)
    slot_cache = jnp.transpose(arrived[:, 64:].reshape(32, 4, 16, 128), (0, 2, 1, 3))

    sel_key = jnp.where(row_pos // DOC_LEN == mine, row_pos % DOC_LEN, -1)
    hits = sel_key[None, :] == jnp.arange(DOC_LEN, dtype=jnp.int32)[:, None]
    covered = jnp.any(hits, axis=1)
    new_own, new_others = own[:, 64:], others[:, 64:]
    new_flat = jnp.stack(
        [jnp.where(c == 0, new_own, new_others), jnp.where(c == 0, new_others, new_own)]
    ).reshape(2, 8, 2, 32, 128)
    new_flat = jnp.transpose(new_flat, (1, 3, 2, 0, 4)).reshape(ROWS, 512)
    placed = jnp.dot(hits.astype(BF), new_flat, preferred_element_type=F32).astype(BF)
    joined = jnp.where(covered[:, None], placed, slot_cache.reshape(DOC_LEN, 512))
    joined = joined.reshape(DOC_LEN, 2, 256)
    result = permute_xy((mid + summed).astype(BF), lambda a, b: (b, a))
    return (result, joined)


def solution(mesh):
    split = Mesh(mesh.devices.reshape(NZ, NX, NC, NY), ("z", "x", "c", "y"))
    pool = ("z", "x", "c")
    return jax.shard_map(
        shards,
        mesh=split,
        in_specs=(
            P(None, pool),
            P(None, pool, None, "y"),
            P(),
            P(),
            P(pool),
            P(pool, "y"),
            P(pool, None, "y"),
            P("y", pool),
            P(pool),
            P(None, None, ("z", "x", "c", "y")),
            P(("z", "x", "c", "y"), None),
        ),
        out_specs=(P("y", pool), P(pool, None, "y")),
        check_vma=False,
    )
```
